128 devices in a mesh: row: 8 (over x_lo, z), col: 16 (over y, x_hi, core).
Axes of the slice: x: 4 (x_hi: 2, x_lo: 2; x = x_hi * 2 + x_lo), y: 4, z: 4, core: 2. Of those that a mesh axis runs over, the one named last changes fastest.
Arguments:
- features: bfloat16 [128, 32768], P('col', 'row'), may hold values from -6 to 6
- weight: bfloat16 [128, 256], P('col'), may hold values from -0.5 to 0.5
- cotangent: bfloat16 [256, 32768], P('col', 'row'), may hold values from -6 to 6
- adjacency: bfloat16 [5120, 128, 128], P('row')
- tile_rows: int32 [5120], P('row'), may hold values from 0 to 31
- tile_cols: int32 [5120], P('row'), may hold values from 0 to 255, as said below
- tile_count: int32 [8], P('row'), may hold values from 160 to 640, as said below
- node_count: int32 [8], P('row'), may hold values from 2048 to 4096, as said below
Outputs:
- hidden_out: bfloat16 [256, 32768], P('col', 'row')
- grad_weight: float32 [128, 256], P('col')
- grad_features: bfloat16 [128, 32768], P('col', 'row')
The draws below stay inside these ranges and needn't reach their ends.
Inputs may be any that keep to these rules, and one draw needn't show every extreme that they name: tile_count[b] is the number of used slots of row block b, the first ones of its 640 slots; some row block uses all 640. `tile_cols`: over the used slots of one row block the column tiles never fall. node_count[b] real nodes lead row block b, the rest are padding; some row block is full.
All inputs are finite; a program needn't handle non-finite values.
Results may differ from the reference program's by a relative error of at most 0.0049.
Values may be sent and summed in bfloat16 or wider, within the bound.
A program may use at most 128 MiB of HBM per device.

```python
import jax
import jax.numpy as jnp
from jax import lax

F = 128
HID = 256
TILE = 128
NODES_DEV = 4096
MAXT = 640
BLOCKS = 8
NODES = 32768
TB = 32
NT = 256
SLOTS = 5120


def shared_counts(key):
    base = jax.random.randint(jax.random.fold_in(key, 101), (BLOCKS,), MAXT // 4, MAXT // 2 + 1)
    fullest = jax.random.randint(jax.random.fold_in(key, 103), (), 0, BLOCKS)
    return jnp.where(jnp.arange(BLOCKS) == fullest, MAXT, base).astype(jnp.int32)


def draw_tile_count(key, part):
    counts = shared_counts(key)
    return counts


def draw_tile_cols(key, part):
    counts = shared_counts(key)
    key = jax.random.fold_in(key, 7)
    raw_cols = jax.random.randint(key, (BLOCKS, MAXT), 0, NT)
    slot_index = jnp.arange(MAXT)[None, :]
    ordered = jnp.sort(jnp.where(slot_index < counts[:, None], raw_cols, raw_cols + NT), axis=1)
    return jnp.where(ordered >= NT, ordered - NT, ordered).reshape(BLOCKS * MAXT).astype(jnp.int32)


def draw_node_count(key, part):
    key = jax.random.fold_in(key, 9)
    base = jax.random.randint(jax.random.fold_in(key, 1), (BLOCKS,), NODES_DEV // 2, NODES_DEV + 1)
    fullest = jax.random.randint(jax.random.fold_in(key, 2), (), 0, BLOCKS)
    return jnp.where(jnp.arange(BLOCKS) == fullest, NODES_DEV, base).astype(jnp.int32)


def draw_adjacency(key, part):
    key = jax.random.fold_in(key, 17)
    first_key, second_key = jax.random.split(key)
    shape = (SLOTS, TILE, TILE)
    factor = (10.1 * MAXT / TB) ** (-0.5)
    present = jax.random.bernoulli(second_key, 0.5, shape).astype(jnp.float32)
    values = jax.random.uniform(first_key, shape, jnp.float32, 0.05, 1.0) * present * factor
    return values.astype(jnp.bfloat16)


def with_ends(result, key, low, high):
    spot = [jax.random.randint(jax.random.fold_in(key, axis), (), 0, length) for axis, length in enumerate(result.shape)]
    widest = result.shape.index(max(result.shape))
    next_to = spot[:widest] + [(spot[widest] + 1) % result.shape[widest]] + spot[widest + 1:]
    return result.at[tuple(spot)].set(low).at[tuple(next_to)].set(high)


def shard_levels(stream_key, shape, pieces, smallest, high):
    def one(dim, parts):
        steps = jax.random.uniform(jax.random.fold_in(jax.random.fold_in(stream_key, 6), dim), (parts,), jnp.float32, smallest / len(pieces), high / len(pieces))
        return jnp.repeat(jnp.exp(steps), shape[dim] // parts).reshape((-1,) + (1,) * (len(shape) - dim - 1))

    level = one(*pieces[0])
    for cut in pieces[1:]:
        level = level * one(*cut)
    return level


def bell_draw(own_key, dims, width, bound, cuts=(), held_as=jnp.bfloat16):
    values = jax.random.normal(own_key, dims, jnp.float32) * width
    if len(cuts) > 0:
        values = shard_levels(own_key, dims, cuts, -0.22, 0.18) * values
    return jnp.clip(values, min=-bound, max=bound).astype(held_as)


def setup_inputs(seed: int = 0) -> dict:
    key_list = jax.random.split(jax.random.key(seed), 9)
    features = bell_draw(key_list[0], (F, NODES), 1.0, 6.0, ((0, 16), (1, 8)))
    weight = bell_draw(key_list[1], (F, HID), F ** -0.5, 0.5, ((0, 16),))
    cotangent = bell_draw(key_list[2], (HID, NODES), 1.0, 6.0, ((0, 16), (1, 8)))
    adjacency = draw_adjacency(jax.random.fold_in(key_list[8], 71), 0)
    tile_rows = with_ends(jax.random.randint(key_list[4], (SLOTS,), 0, TB), jax.random.fold_in(key_list[4], 1), 0, TB - 1).astype(jnp.int32)
    tile_cols = draw_tile_cols(jax.random.fold_in(key_list[8], 71), 0)
    tile_count = draw_tile_count(jax.random.fold_in(key_list[8], 71), 0)
    node_count = draw_node_count(jax.random.fold_in(key_list[8], 71), 0)
    return {"features": features, "weight": weight, "cotangent": cotangent, "adjacency": adjacency, "tile_rows": tile_rows, "tile_cols": tile_cols, "tile_count": tile_count, "node_count": node_count}


def reference(features, weight, cotangent, adjacency, tile_rows, tile_cols, tile_count, node_count):
    living = (jnp.arange(NODES_DEV)[None, :] < node_count[:, None]).reshape(NODES)
    masked = jnp.where(living[None, :], features, jnp.zeros_like(features))
    source_blocks = masked.reshape(F, NT, TILE)
    in_use = jnp.arange(MAXT)[None, :] < tile_count[:, None]
    tiles_by_block = adjacency.reshape(BLOCKS, MAXT, TILE, TILE)
    rows_by_block = tile_rows.reshape(BLOCKS, MAXT)
    cols_by_block = tile_cols.reshape(BLOCKS, MAXT)

    def forward_block(operands):
        block_tiles, block_rows, block_cols, block_use = operands
        sources = jnp.take(source_blocks, block_cols, axis=1).astype(jnp.float32)
        products = jnp.einsum("fgm,gnm->gfn", sources, block_tiles.astype(jnp.float32))
        placing = ((block_rows[:, None] == jnp.arange(TB)[None, :]) & block_use[:, None]).astype(jnp.float32)
        return jnp.einsum("gi,gfn->fin", placing, products).reshape(F, NODES_DEV)

    summed = lax.map(forward_block, (tiles_by_block, rows_by_block, cols_by_block, in_use))
    summed = jnp.transpose(summed, (1, 0, 2)).reshape(F, NODES)
    aggregate = jnp.where(living[None, :], summed, 0.0).astype(jnp.bfloat16)
    hidden_out = jnp.dot(weight.T, aggregate, preferred_element_type=jnp.float32).astype(jnp.bfloat16)
    grad_weight = jnp.dot(aggregate, cotangent.T, preferred_element_type=jnp.float32) * (float(NODES) ** -0.5)
    back_sum = jnp.dot(weight, cotangent, preferred_element_type=jnp.float32)
    back_rows = jnp.where(living[None, :], back_sum, 0.0).astype(jnp.bfloat16)
    back_blocks = jnp.transpose(back_rows.reshape(F, BLOCKS, TB, TILE), (1, 0, 2, 3))

    def backward_block(running, operands):
        block_tiles, block_rows, block_cols, block_use, block_back = operands
        sources = jnp.take(block_back, block_rows, axis=1).astype(jnp.float32)
        products = jnp.einsum("fgn,gnm->gfm", sources, block_tiles.astype(jnp.float32))
        placing = ((block_cols[:, None] == jnp.arange(NT)[None, :]) & block_use[:, None]).astype(jnp.float32)
        return running + jnp.einsum("gj,gfm->fjm", placing, products), None

    grad_sum, _ = lax.scan(backward_block, jnp.zeros((F, NT, TILE), jnp.float32),
                           (tiles_by_block, rows_by_block, cols_by_block, in_use, back_blocks))
    grad_features = jnp.where(living[None, :], grad_sum.reshape(F, NODES), 0.0).astype(jnp.bfloat16)
    return (hidden_out, grad_weight, grad_features)
```

```python
import functools

import jax
import jax.numpy as jnp
from jax import lax
from jax.experimental import pallas as pl
from jax.experimental.pallas import tpu as pltpu
from jax.sharding import PartitionSpec as P

TILE = 128
MESH = pl.DeviceIdType.MESH
NT = (((1,), (1,)), ((), ()))
NN = (((1,), (0,)), ((), ()))
BF = jnp.bfloat16
F32 = jnp.float32


def kernel(
    rows, cols, slots, chunks, unroll,
    feat_ref, weight_ref, cot_ref, adj_hbm, trow_s, tcol_s, trow_v, tcol_v, tcount, ncount,
    hid_ref, gw_ref, gf_ref,
    adj, fstage, fgath, cgath, wstage, wgath, bstage, bgath, prod, sums, gstage, ggath,
    astage, agath, hstage, wpart, wpgath, wrow, wrgath, chosen_c, chosen_r,
    adj_sem, own_sem, send_sem, recv_sem,
):
    me_r = lax.axis_index("row")
    me_c = lax.axis_index("col")
    tiles_dev = 2 * cols
    node_total = rows * tiles_dev * TILE
    per_chunk = slots // chunks

    def adj_copy(i):
        part = pl.ds(i * per_chunk, per_chunk)
        return pltpu.make_async_copy(adj_hbm.at[part], adj.at[part], adj_sem.at[i])

    for i in range(chunks):
        adj_copy(i).start()

    barrier = pltpu.get_barrier_semaphore()

    def greet_row(k, carry):
        pl.semaphore_signal(barrier, inc=1, device_id=(lax.rem(me_r + k, rows), me_c), device_id_type=MESH)
        return carry

    def greet_col(k, carry):
        pl.semaphore_signal(barrier, inc=1, device_id=(me_r, lax.rem(me_c + k, cols)), device_id_type=MESH)
        return carry

    lax.fori_loop(1, rows, greet_row, 0)
    lax.fori_loop(1, cols, greet_col, 0)

    live_count = ncount[0]
    used = tcount[0]

    lane = lax.broadcasted_iota(jnp.int32, (8, TILE), 1)
    for p in range(cols):
        halves = []
        for h in range(2):
            at = (2 * p + h) * TILE
            block = feat_ref[:, at:at + TILE].astype(F32)
            halves.append(jnp.where(lane + at < live_count, block, 0.0))
        fstage[p] = jnp.concatenate(halves, axis=0).astype(BF)
    wstage[...] = weight_ref[...].astype(F32)

    pl.semaphore_wait(barrier, rows + cols - 2)

    def to_col(phase, source, target):
        def one(k, carry):
            peer = lax.rem(me_c + k, cols)
            pltpu.make_async_remote_copy(
                src_ref=source(peer), dst_ref=target, send_sem=send_sem.at[phase], recv_sem=recv_sem.at[phase],
                device_id=(me_r, peer), device_id_type=MESH,
            ).start()
            return carry

        lax.fori_loop(1, cols, one, 0)

    def to_row(phase, source, target):
        def one(k, carry):
            peer = lax.rem(me_r + k, rows)
            pltpu.make_async_remote_copy(
                src_ref=source(peer), dst_ref=target, send_sem=send_sem.at[phase], recv_sem=recv_sem.at[phase],
                device_id=(peer, me_c), device_id_type=MESH,
            ).start()
            return carry

        lax.fori_loop(1, rows, one, 0)

    def arrived(phase, ref):
        pltpu.make_async_copy(ref, ref, recv_sem.at[phase]).wait()

    def sent(phase, ref):
        pltpu.make_async_copy(ref, ref, send_sem.at[phase]).wait()

    def slice_cols(index):
        return pl.ds(pl.multiple_of(index * 2 * TILE, 2 * TILE), 2 * TILE)

    to_col(0, lambda d: cot_ref.at[:, slice_cols(d)], cgath.at[me_c])
    to_col(1, lambda d: wstage, wgath.at[me_c])
    to_row(2, lambda d: fstage, fgath.at[me_r])
    own_c = pltpu.make_async_copy(cot_ref.at[:, slice_cols(me_c)], cgath.at[me_c], own_sem.at[0])
    own_w = pltpu.make_async_copy(wstage, wgath.at[me_c], own_sem.at[1])
    own_f = pltpu.make_async_copy(fstage, fgath.at[me_r], own_sem.at[2])
    own_c.start()
    own_w.start()
    own_f.start()

    slot_used = lax.broadcasted_iota(jnp.int32, (1, slots), 1) < used
    key_c = jnp.where(slot_used, tcol_v[...], -1)
    key_r = jnp.where(slot_used, trow_v[...], -1)
    chosen_c[...] = (
        lax.broadcasted_iota(jnp.int32, (rows * tiles_dev, slots), 0) == key_c
    ).astype(F32).astype(BF)
    chosen_r[...] = (lax.broadcasted_iota(jnp.int32, (tiles_dev, slots), 0) == key_r).astype(F32).astype(BF)

    own_c.wait()
    own_w.wait()
    arrived(0, cgath.at[pl.ds(0, cols - 1)])
    arrived(1, wgath.at[pl.ds(0, cols - 1)])
    whole_w = wgath[...].reshape(cols * 8, -1).astype(BF)
    cot_nodes = cgath[...].reshape(cols * 16, 2 * TILE)
    back = lax.dot_general(whole_w, cot_nodes, NN, preferred_element_type=F32)
    node = lax.broadcasted_iota(jnp.int32, back.shape, 1) + me_c * (2 * TILE)
    back = jnp.where(node < live_count, back, 0.0)
    for d in range(cols):
        part = back[8 * d:8 * d + 8]
        bstage[d] = jnp.concatenate([part[:, :TILE], part[:, TILE:]], axis=0).astype(BF)
    to_col(3, lambda d: bstage.at[d], bgath.at[me_c])
    own_b = pltpu.make_async_copy(bstage.at[me_c], bgath.at[me_c], own_sem.at[3])
    own_b.start()
    own_b.wait()
    arrived(3, bgath.at[pl.ds(0, cols - 1)])

    zero = jnp.zeros((16, TILE), BF)

    def tile_pass(source, index_s, forward):
        group = 4 * unroll

        def step(g, carry):
            for u in range(unroll):
                s = pl.multiple_of(g * group, group) + 4 * u
                at = [index_s[s + i] for i in range(4)]
                x = [source[at[i] // 2] for i in range(4)]
                spread = (
                    [[x[0], zero], [x[1], zero], [zero, x[2]], [zero, x[3]]]
                    if forward
                    else [[x[0], zero], [zero, x[1]], [x[2], zero], [zero, x[3]]]
                )
                left = jnp.concatenate([jnp.concatenate(pair, axis=1) for pair in spread], axis=0)
                right = jnp.concatenate(
                    [adj[pl.ds(s, 2)].reshape(2 * TILE, TILE), adj[pl.ds(s + 2, 2)].reshape(2 * TILE, TILE)], axis=1
                )
                out = lax.dot_general(left, right, NT if forward else NN, preferred_element_type=F32)
                for i in range(4):
                    half = i % 2 if forward else i // 2
                    block = out[16 * i:16 * i + 16, TILE * half:TILE * half + TILE]
                    block = jnp.where(at[i] % 2 == 0, block[:8], block[8:])
                    block = jnp.where(s + i < used, block, 0.0)
                    prod[pl.ds(pl.multiple_of((s + i) * 8, 8), 8), :] = block
            return carry

        return step

    def add_up(chosen, tiles):
        picks = chosen[...]
        for f in range(0, 8, 2):
            pair = jnp.concatenate([prod[pl.ds(f + j, slots, stride=8), :] for j in range(2)], axis=1)
            high = pair.astype(BF)
            low = (pair - high.astype(F32)).astype(BF)
            total = lax.dot_general(picks, high, NN, preferred_element_type=F32) + lax.dot_general(
                picks, low, NN, preferred_element_type=F32
            )
            for j in range(2):
                sums[pl.ds(f + j, tiles, stride=8), :] = total[:, TILE * j:TILE * j + TILE]

    groups = slots // (4 * unroll)
    per_group = chunks // groups if chunks > groups else 1

    def backward_step(g, carry):
        adj_copy(g).wait()
        return tile_pass(bgath, trow_s, False)(g, carry)

    lax.fori_loop(0, groups, backward_step, 0)
    add_up(chosen_c, rows * tiles_dev)
    for d in range(rows):
        size = tiles_dev * 8
        gstage[d] = sums[d * size:(d + 1) * size, :].reshape(cols, 16, TILE).astype(BF)
    to_row(4, lambda d: gstage.at[d], ggath.at[me_r])
    own_g = pltpu.make_async_copy(gstage.at[me_r], ggath.at[me_r], own_sem.at[4])
    own_g.start()

    own_f.wait()
    arrived(2, fgath.at[pl.ds(0, rows - 1)])
    features = fgath.reshape(rows * cols, 16, TILE)
    lax.fori_loop(0, groups, tile_pass(features, tcol_s, True), 0)
    add_up(chosen_r, tiles_dev)
    for d in range(cols):
        halves = []
        for h in range(2):
            at = 2 * d + h
            block = sums[8 * at:8 * at + 8, :]
            halves.append(jnp.where(lane + at * TILE < live_count, block, 0.0))
        astage[d] = jnp.concatenate(halves, axis=0).astype(BF)
    to_col(5, lambda d: astage.at[d], agath.at[me_c])
    own_a = pltpu.make_async_copy(astage.at[me_c], agath.at[me_c], own_sem.at[5])
    own_a.start()
    own_a.wait()
    arrived(5, agath.at[pl.ds(0, cols - 1)])

    spread = agath[...].astype(F32)
    agg = jnp.concatenate(
        [spread[:, :8].reshape(cols * 8, TILE), spread[:, 8:].reshape(cols * 8, TILE)], axis=1
    ).astype(BF)
    gw = lax.dot_general(agg, cgath[...].reshape(cols * 16, 2 * TILE), NT, preferred_element_type=F32)
    wpart[...] = gw.reshape(cols, 8, gw.shape[1])
    to_col(6, lambda d: wpart.at[d], wpgath.at[me_c])
    whole_w = wgath[...].reshape(cols * 8, -1).astype(BF)
    hidden = lax.dot_general(whole_w, agg, (((0,), (0,)), ((), ())), preferred_element_type=F32)
    hstage[...] = hidden.astype(BF).reshape(cols, 16, 2 * TILE)
    to_col(7, lambda d: hstage.at[d], hid_ref.at[:, slice_cols(me_c)])
    own_h = pltpu.make_async_copy(hstage.at[me_c], hid_ref.at[:, slice_cols(me_c)], own_sem.at[6])
    own_h.start()
    own_p = pltpu.make_async_copy(wpart.at[me_c], wpgath.at[me_c], own_sem.at[7])
    own_p.start()

    own_g.wait()
    arrived(4, ggath.at[pl.ds(0, rows - 1)])
    for p in range(cols):
        total = ggath[0, p].astype(F32)
        for d in range(1, rows):
            total = total + ggath[d, p].astype(F32)
        for h in range(2):
            at = (2 * p + h) * TILE
            gf_ref[:, at:at + TILE] = jnp.where(lane + at < live_count, total[8 * h:8 * h + 8], 0.0).astype(BF)

    own_p.wait()
    arrived(6, wpgath.at[pl.ds(0, cols - 1)])
    wrow[...] = jnp.sum(wpgath[...], axis=0)
    to_row(8, lambda d: wrow, wrgath.at[me_r])
    own_r = pltpu.make_async_copy(wrow, wrgath.at[me_r], own_sem.at[8])
    own_r.start()
    own_r.wait()
    arrived(8, wrgath.at[pl.ds(0, rows - 1)])
    total = wrgath[0]
    for d in range(1, rows):
        total = total + wrgath[d]
    gw_ref[...] = total * float(node_total) ** (-0.5)

    own_h.wait()
    arrived(7, hstage.at[pl.ds(0, cols - 1)])
    sent(0, cgath.at[pl.ds(0, cols - 1)])
    sent(1, wgath.at[pl.ds(0, cols - 1)])
    sent(2, fgath.at[pl.ds(0, rows - 1)])
    sent(3, bgath.at[pl.ds(0, cols - 1)])
    sent(4, ggath.at[pl.ds(0, rows - 1)])
    sent(5, agath.at[pl.ds(0, cols - 1)])
    sent(6, wpgath.at[pl.ds(0, cols - 1)])
    sent(7, hstage.at[pl.ds(0, cols - 1)])
    sent(8, wrgath.at[pl.ds(0, rows - 1)])


def solution(mesh):
    rows, cols = mesh.shape["row"], mesh.shape["col"]

    def local(features, weight, cotangent, adjacency, tile_rows, tile_cols, tile_count, node_count):
        slots = adjacency.shape[0]
        feats, nodes = features.shape
        hid = weight.shape[1]
        tiles = nodes // TILE
        unroll = 20
        groups = slots // (4 * unroll)
        smem = pl.BlockSpec(memory_space=pltpu.SMEM)
        vmem = pl.BlockSpec(memory_space=pltpu.VMEM)
        return pl.pallas_call(
            functools.partial(kernel, rows, cols, slots, groups, unroll),
            out_shape=(
                jax.ShapeDtypeStruct(cotangent.shape, BF),
                jax.ShapeDtypeStruct(weight.shape, F32),
                jax.ShapeDtypeStruct(features.shape, BF),
            ),
            in_specs=[vmem, vmem, vmem, pl.BlockSpec(memory_space=pl.ANY), smem, smem, vmem, vmem, smem, smem],
            out_specs=(vmem, vmem, vmem),
            scratch_shapes=[
                pltpu.VMEM((slots, TILE, TILE), BF),
                pltpu.VMEM((cols, 16, TILE), BF),
                pltpu.VMEM((rows, cols, 16, TILE), BF),
                pltpu.VMEM((cols, 16, 2 * TILE), BF),
                pltpu.VMEM((8, hid), F32),
                pltpu.VMEM((cols, 8, hid), F32),
                pltpu.VMEM((cols, 16, TILE), BF),
                pltpu.VMEM((cols, 16, TILE), BF),
                pltpu.VMEM((slots * 8, TILE), F32),
                pltpu.VMEM((rows * tiles * 8, TILE), F32),
                pltpu.VMEM((rows, cols, 16, TILE), BF),
                pltpu.VMEM((rows, cols, 16, TILE), BF),
                pltpu.VMEM((cols, 16, TILE), BF),
                pltpu.VMEM((cols, 16, TILE), BF),
                pltpu.VMEM((cols, 16, 2 * TILE), BF),
                pltpu.VMEM((cols, 8, hid), F32),
                pltpu.VMEM((cols, 8, hid), F32),
                pltpu.VMEM((8, hid), F32),
                pltpu.VMEM((rows, 8, hid), F32),
                pltpu.VMEM((rows * tiles, slots), BF),
                pltpu.VMEM((tiles, slots), BF),
                pltpu.SemaphoreType.DMA((groups,)),
                pltpu.SemaphoreType.DMA((9,)),
                pltpu.SemaphoreType.DMA((9,)),
                pltpu.SemaphoreType.DMA((9,)),
            ],
            compiler_params=pltpu.CompilerParams(
                collective_id=0, has_side_effects=True, vmem_limit_bytes=60 * 2**20
            ),
        )(
            features, weight, cotangent, adjacency, tile_rows, tile_cols,
            tile_rows.reshape(1, slots), tile_cols.reshape(1, slots), tile_count, node_count,
        )

    return jax.shard_map(
        local,
        mesh=mesh,
        in_specs=(
            P("col", "row"), P("col", None), P("col", "row"), P("row", None, None),
            P("row"), P("row"), P("row"), P("row"),
        ),
        out_specs=(P("col", "row"), P("col", None), P("col", "row")),
        check_vma=False,
    )
```

```python
import functools

import jax
import jax.numpy as jnp
from jax import lax
from jax.experimental import pallas as pl
from jax.experimental.pallas import tpu as pltpu
from jax.sharding import PartitionSpec as P

TILE = 128
MESH = pl.DeviceIdType.MESH
NT = (((1,), (1,)), ((), ()))
NN = (((1,), (0,)), ((), ()))
BF = jnp.bfloat16
F32 = jnp.float32


def kernel(
    rows, cols, slots, chunks, unroll,
    feat_hbm, weight_hbm, cot_hbm, adj_hbm, trow_s, tcol_s, trow_v, tcol_v, tcount, ncount,
    hid_ref, gw_ref, gf_ref,
    feat_ref, weight_ref, cot_ref, adj, fstage, fgath, cgath, wstage, wgath, bstage, bgath, prod, sums, gstage, ggath,
    astage, agath, hstage, wpart, wpgath, wrow, wrgath, chosen_c, chosen_r,
    adj_sem, in_sem, own_sem, send_sem, recv_sem,
):
    me_r = lax.axis_index("row")
    me_c = lax.axis_index("col")
    tiles_dev = 2 * cols
    node_total = rows * tiles_dev * TILE
    per_chunk = slots // chunks

    def adj_copy(i):
        part = pl.ds(i * per_chunk, per_chunk)
        return pltpu.make_async_copy(adj_hbm.at[part], adj.at[part], adj_sem.at[i])


    barrier = pltpu.get_barrier_semaphore()

    def greet_row(k, carry):
        pl.semaphore_signal(barrier, inc=1, device_id=(lax.rem(me_r + k, rows), me_c), device_id_type=MESH)
        return carry

    def greet_col(k, carry):
        pl.semaphore_signal(barrier, inc=1, device_id=(me_r, lax.rem(me_c + k, cols)), device_id_type=MESH)
        return carry

    lax.fori_loop(1, rows, greet_row, 0)
    lax.fori_loop(1, cols, greet_col, 0)

    inputs = [
        pltpu.make_async_copy(feat_hbm, feat_ref, in_sem.at[0]),
        pltpu.make_async_copy(cot_hbm, cot_ref, in_sem.at[1]),
        pltpu.make_async_copy(weight_hbm, weight_ref, in_sem.at[2]),
    ]
    for copy in inputs:
        copy.start()
    for i in range(chunks):
        adj_copy(i).start()

    live_count = ncount[0]
    used = tcount[0]

    lane = lax.broadcasted_iota(jnp.int32, (8, TILE), 1)
    for copy in inputs:
        copy.wait()
    for p in range(cols):
        halves = []
        for h in range(2):
            at = (2 * p + h) * TILE
            block = feat_ref[:, at:at + TILE].astype(F32)
            halves.append(jnp.where(lane + at < live_count, block, 0.0))
        fstage[p] = jnp.concatenate(halves, axis=0).astype(BF)
    wstage[...] = weight_ref[...].astype(F32)

    pl.semaphore_wait(barrier, rows + cols - 2)

    def to_col(phase, source, target):
        def one(k, carry):
            peer = lax.rem(me_c + k, cols)
            pltpu.make_async_remote_copy(
                src_ref=source(peer), dst_ref=target, send_sem=send_sem.at[phase], recv_sem=recv_sem.at[phase],
                device_id=(me_r, peer), device_id_type=MESH,
            ).start()
            return carry

        lax.fori_loop(1, cols, one, 0)

    def to_row(phase, source, target):
        def one(k, carry):
            peer = lax.rem(me_r + k, rows)
            pltpu.make_async_remote_copy(
                src_ref=source(peer), dst_ref=target, send_sem=send_sem.at[phase], recv_sem=recv_sem.at[phase],
                device_id=(peer, me_c), device_id_type=MESH,
            ).start()
            return carry

        lax.fori_loop(1, rows, one, 0)

    def arrived(phase, ref):
        pltpu.make_async_copy(ref, ref, recv_sem.at[phase]).wait()

    def sent(phase, ref):
        pltpu.make_async_copy(ref, ref, send_sem.at[phase]).wait()

    def slice_cols(index):
        return pl.ds(pl.multiple_of(index * 2 * TILE, 2 * TILE), 2 * TILE)

    to_col(0, lambda d: cot_ref.at[:, slice_cols(d)], cgath.at[me_c])
    to_col(1, lambda d: wstage, wgath.at[me_c])
    to_row(2, lambda d: fstage, fgath.at[me_r])
    own_c = pltpu.make_async_copy(cot_ref.at[:, slice_cols(me_c)], cgath.at[me_c], own_sem.at[0])
    own_w = pltpu.make_async_copy(wstage, wgath.at[me_c], own_sem.at[1])
    own_f = pltpu.make_async_copy(fstage, fgath.at[me_r], own_sem.at[2])
    own_c.start()
    own_w.start()
    own_f.start()

    slot_used = lax.broadcasted_iota(jnp.int32, (1, slots), 1) < used
    key_c = jnp.where(slot_used, tcol_v[...].reshape(1, slots), -1)
    key_r = jnp.where(slot_used, trow_v[...].reshape(1, slots), -1)
    chosen_c[...] = (
        lax.broadcasted_iota(jnp.int32, (rows * tiles_dev, slots), 0) == key_c
    ).astype(F32).astype(BF)
    chosen_r[...] = (lax.broadcasted_iota(jnp.int32, (tiles_dev, slots), 0) == key_r).astype(F32).astype(BF)

    own_c.wait()
    own_w.wait()
    arrived(0, cgath.at[pl.ds(0, cols - 1)])
    arrived(1, wgath.at[pl.ds(0, cols - 1)])
    whole_w = wgath[...].reshape(cols * 8, -1).astype(BF)
    cot_nodes = cgath[...].reshape(cols * 16, 2 * TILE)
    back = lax.dot_general(whole_w, cot_nodes, NN, preferred_element_type=F32)
    node = lax.broadcasted_iota(jnp.int32, back.shape, 1) + me_c * (2 * TILE)
    back = jnp.where(node < live_count, back, 0.0)
    for d in range(cols):
        part = back[8 * d:8 * d + 8]
        bstage[d] = jnp.concatenate([part[:, :TILE], part[:, TILE:]], axis=0).astype(BF)
    to_col(3, lambda d: bstage.at[d], bgath.at[me_c])
    own_b = pltpu.make_async_copy(bstage.at[me_c], bgath.at[me_c], own_sem.at[3])
    own_b.start()
    zero = jnp.zeros((16, TILE), BF)

    def tile_pass(source, index_s, forward):
        group = 4 * unroll

        def step(g, carry):
            for u in range(unroll):
                s = pl.multiple_of(g * group, group) + 4 * u
                at = [index_s[s + i] for i in range(4)]
                x = [source[at[i] // 2] for i in range(4)]
                spread = (
                    [[x[0], zero], [x[1], zero], [zero, x[2]], [zero, x[3]]]
                    if forward
                    else [[x[0], zero], [zero, x[1]], [x[2], zero], [zero, x[3]]]
                )
                left = jnp.concatenate([jnp.concatenate(pair, axis=1) for pair in spread], axis=0)
                right = jnp.concatenate(
                    [adj[pl.ds(s, 2)].reshape(2 * TILE, TILE), adj[pl.ds(s + 2, 2)].reshape(2 * TILE, TILE)], axis=1
                )
                out = lax.dot_general(left, right, NT if forward else NN, preferred_element_type=F32)
                for i in range(4):
                    half = i % 2 if forward else i // 2
                    block = out[16 * i:16 * i + 16, TILE * half:TILE * half + TILE]
                    block = jnp.where(at[i] % 2 == 0, block[:8], block[8:])
                    block = jnp.where(s + i < used, block, 0.0)
                    prod[pl.ds(pl.multiple_of((s + i) * 8, 8), 8), :] = block
            return carry

        return step

    def add_up(chosen, tiles):
        picks = chosen[...]
        for f in range(0, 8, 2):
            pair = jnp.concatenate([prod[pl.ds(f + j, slots, stride=8), :] for j in range(2)], axis=1)
            high = pair.astype(BF)
            low = (pair - high.astype(F32)).astype(BF)
            total = lax.dot_general(picks, high, NN, preferred_element_type=F32) + lax.dot_general(
                picks, low, NN, preferred_element_type=F32
            )
            for j in range(2):
                sums[pl.ds(f + j, tiles, stride=8), :] = total[:, TILE * j:TILE * j + TILE]

    own_f.wait()
    arrived(2, fgath.at[pl.ds(0, rows - 1)])
    features = fgath.reshape(rows * cols, 16, TILE)
    groups = slots // (4 * unroll)
    forward = tile_pass(features, tcol_s, True)

    def forward_step(g, carry):
        adj_copy(g).wait()
        return forward(g, carry)

    lax.fori_loop(0, groups, forward_step, 0)
    add_up(chosen_r, tiles_dev)
    for d in range(cols):
        halves = []
        for h in range(2):
            at = 2 * d + h
            block = sums[8 * at:8 * at + 8, :]
            halves.append(jnp.where(lane + at * TILE < live_count, block, 0.0))
        astage[d] = jnp.concatenate(halves, axis=0).astype(BF)
    to_col(5, lambda d: astage.at[d], agath.at[me_c])
    own_a = pltpu.make_async_copy(astage.at[me_c], agath.at[me_c], own_sem.at[5])
    own_a.start()
    own_b.wait()
    arrived(3, bgath.at[pl.ds(0, cols - 1)])

    backward = tile_pass(bgath, trow_s, False)
    lax.fori_loop(0, groups - 1, backward, 0)
    own_a.wait()
    arrived(5, agath.at[pl.ds(0, cols - 1)])

    spread = agath[...].astype(F32)
    agg = jnp.concatenate(
        [spread[:, :8].reshape(cols * 8, TILE), spread[:, 8:].reshape(cols * 8, TILE)], axis=1
    ).astype(BF)
    gw = lax.dot_general(agg, cgath[...].reshape(cols * 16, 2 * TILE), NT, preferred_element_type=F32)
    wpart[...] = gw.reshape(cols, 8, gw.shape[1])
    to_col(6, lambda d: wpart.at[d], wpgath.at[me_c])
    whole_w = wgath[...].reshape(cols * 8, -1).astype(BF)
    hidden = lax.dot_general(whole_w, agg, (((0,), (0,)), ((), ())), preferred_element_type=F32)
    hstage[...] = hidden.astype(BF).reshape(cols, 16, 2 * TILE)
    to_col(7, lambda d: hstage.at[d], hid_ref.at[:, slice_cols(me_c)])
    own_h = pltpu.make_async_copy(hstage.at[me_c], hid_ref.at[:, slice_cols(me_c)], own_sem.at[6])
    own_h.start()
    own_p = pltpu.make_async_copy(wpart.at[me_c], wpgath.at[me_c], own_sem.at[7])
    own_p.start()

    lax.fori_loop(groups - 1, groups, backward, 0)
    add_up(chosen_c, rows * tiles_dev)
    for d in range(rows):
        size = tiles_dev * 8
        gstage[d] = sums[d * size:(d + 1) * size, :].reshape(cols, 16, TILE).astype(BF)
    to_row(4, lambda d: gstage.at[d], ggath.at[me_r])
    own_g = pltpu.make_async_copy(gstage.at[me_r], ggath.at[me_r], own_sem.at[4])
    own_g.start()

    own_p.wait()
    arrived(6, wpgath.at[pl.ds(0, cols - 1)])
    wrow[...] = jnp.sum(wpgath[...], axis=0)
    to_row(8, lambda d: wrow, wrgath.at[me_r])
    own_r = pltpu.make_async_copy(wrow, wrgath.at[me_r], own_sem.at[8])
    own_r.start()
    own_g.wait()
    arrived(4, ggath.at[pl.ds(0, rows - 1)])
    for p in range(cols):
        total = ggath[0, p].astype(F32)
        for d in range(1, rows):
            total = total + ggath[d, p].astype(F32)
        for h in range(2):
            at = (2 * p + h) * TILE
            gf_ref[:, at:at + TILE] = jnp.where(lane + at < live_count, total[8 * h:8 * h + 8], 0.0).astype(BF)

    own_r.wait()
    arrived(8, wrgath.at[pl.ds(0, rows - 1)])
    total = wrgath[0]
    for d in range(1, rows):
        total = total + wrgath[d]
    gw_ref[...] = total * float(node_total) ** (-0.5)

    own_h.wait()
    arrived(7, hstage.at[pl.ds(0, cols - 1)])
    sent(0, cgath.at[pl.ds(0, cols - 1)])
    sent(1, wgath.at[pl.ds(0, cols - 1)])
    sent(2, fgath.at[pl.ds(0, rows - 1)])
    sent(3, bgath.at[pl.ds(0, cols - 1)])
    sent(4, ggath.at[pl.ds(0, rows - 1)])
    sent(5, agath.at[pl.ds(0, cols - 1)])
    sent(6, wpgath.at[pl.ds(0, cols - 1)])
    sent(7, hstage.at[pl.ds(0, cols - 1)])
    sent(8, wrgath.at[pl.ds(0, rows - 1)])


def finish(a_in, b_in, c_in, a_out, b_out, c_out, sems):
    copies = [
        pltpu.make_async_copy(a_in, a_out, sems.at[0]),
        pltpu.make_async_copy(b_in, b_out, sems.at[1]),
        pltpu.make_async_copy(c_in, c_out, sems.at[2]),
    ]
    for copy in copies:
        copy.start()
    for copy in copies:
        copy.wait()


def solution(mesh):
    rows, cols = mesh.shape["row"], mesh.shape["col"]

    def local(features, weight, cotangent, adjacency, tile_rows, tile_cols, tile_count, node_count):
        slots = adjacency.shape[0]
        feats, nodes = features.shape
        hid = weight.shape[1]
        tiles = nodes // TILE
        unroll = 20
        groups = slots // (4 * unroll)
        smem = pl.BlockSpec(memory_space=pltpu.SMEM)
        vmem = pl.BlockSpec(memory_space=pltpu.VMEM)
        anywhere = pl.BlockSpec(memory_space=pl.ANY)
        partial_out = pl.pallas_call(
            functools.partial(kernel, rows, cols, slots, groups, unroll),
            out_shape=(
                jax.ShapeDtypeStruct(cotangent.shape, BF),
                jax.ShapeDtypeStruct(weight.shape, F32),
                jax.ShapeDtypeStruct(features.shape, BF),
            ),
            in_specs=[anywhere] * 4 + [smem, smem, vmem, vmem, smem, smem],
            out_specs=(vmem, vmem, vmem),
            scratch_shapes=[
                pltpu.VMEM(features.shape, BF),
                pltpu.VMEM(weight.shape, BF),
                pltpu.VMEM(cotangent.shape, BF),
                pltpu.VMEM((slots, TILE, TILE), BF),
                pltpu.VMEM((cols, 16, TILE), BF),
                pltpu.VMEM((rows, cols, 16, TILE), BF),
                pltpu.VMEM((cols, 16, 2 * TILE), BF),
                pltpu.VMEM((8, hid), F32),
                pltpu.VMEM((cols, 8, hid), F32),
                pltpu.VMEM((cols, 16, TILE), BF),
                pltpu.VMEM((cols, 16, TILE), BF),
                pltpu.VMEM((slots * 8, TILE), F32),
                pltpu.VMEM((rows * tiles * 8, TILE), F32),
                pltpu.VMEM((rows, cols, 16, TILE), BF),
                pltpu.VMEM((rows, cols, 16, TILE), BF),
                pltpu.VMEM((cols, 16, TILE), BF),
                pltpu.VMEM((cols, 16, TILE), BF),
                pltpu.VMEM((cols, 16, 2 * TILE), BF),
                pltpu.VMEM((cols, 8, hid), F32),
                pltpu.VMEM((cols, 8, hid), F32),
                pltpu.VMEM((8, hid), F32),
                pltpu.VMEM((rows, 8, hid), F32),
                pltpu.VMEM((rows * tiles, slots), BF),
                pltpu.VMEM((tiles, slots), BF),
                pltpu.SemaphoreType.DMA((groups,)),
                pltpu.SemaphoreType.DMA((3,)),
                pltpu.SemaphoreType.DMA((9,)),
                pltpu.SemaphoreType.DMA((9,)),
                pltpu.SemaphoreType.DMA((9,)),
            ],
            compiler_params=pltpu.CompilerParams(
                collective_id=0, has_side_effects=True, vmem_limit_bytes=60 * 2**20
            ),
        )(
            features, weight, cotangent, adjacency, tile_rows, tile_cols,
            tile_rows, tile_cols, tile_count, node_count,
        )
        return pl.pallas_call(
            finish,
            out_shape=[jax.ShapeDtypeStruct(x.shape, x.dtype) for x in partial_out],
            in_specs=[anywhere] * 3,
            out_specs=[anywhere] * 3,
            scratch_shapes=[pltpu.SemaphoreType.DMA((3,))],
        )(*partial_out)

    return jax.shard_map(
        local,
        mesh=mesh,
        in_specs=(
            P("col", "row"), P("col", None), P("col", "row"), P("row", None, None),
            P("row"), P("row"), P("row"), P("row"),
        ),
        out_specs=(P("col", "row"), P("col", None), P("col", "row")),
        check_vma=False,
    )
```

```python
import functools

import jax
import jax.numpy as jnp
from jax import lax
from jax.experimental import pallas as pl
from jax.experimental.pallas import tpu as pltpu
from jax.sharding import PartitionSpec as P

TILE = 128
MESH = pl.DeviceIdType.MESH
NT = (((1,), (1,)), ((), ()))
NN = (((1,), (0,)), ((), ()))
BF = jnp.bfloat16
F32 = jnp.float32


def kernel(
    rows, cols, slots, chunks, unroll,
    feat_hbm, weight_hbm, cot_hbm, adj_hbm, trow_s, tcol_s, trow_v, tcol_v, tcount, ncount,
    hid_ref, gw_ref, gf_ref,
    feat_ref, weight_ref, cot_ref, adj, fstage, fgath, cgath, wstage, wgath, bstage, bgath, prod, sums, gstage, ggath,
    astage, agath, hstage, wpart, wpgath, wrow, wrgath, chosen_c, chosen_r,
    adj_sem, in_sem, own_sem, send_sem, recv_sem,
):
    me_r = lax.axis_index("row")
    me_c = lax.axis_index("col")
    tiles_dev = 2 * cols
    node_total = rows * tiles_dev * TILE
    per_chunk = slots // chunks

    def adj_copy(i):
        part = pl.ds(i * per_chunk, per_chunk)
        return pltpu.make_async_copy(adj_hbm.at[part], adj.at[part], adj_sem.at[i])


    barrier = pltpu.get_barrier_semaphore()

    def greet_row(k, carry):
        pl.semaphore_signal(barrier, inc=1, device_id=(lax.rem(me_r + k, rows), me_c), device_id_type=MESH)
        return carry

    def greet_col(k, carry):
        pl.semaphore_signal(barrier, inc=1, device_id=(me_r, lax.rem(me_c + k, cols)), device_id_type=MESH)
        return carry

    lax.fori_loop(1, rows, greet_row, 0)
    lax.fori_loop(1, cols, greet_col, 0)

    inputs = [
        pltpu.make_async_copy(feat_hbm, feat_ref, in_sem.at[0]),
        pltpu.make_async_copy(cot_hbm, cot_ref, in_sem.at[1]),
        pltpu.make_async_copy(weight_hbm, weight_ref, in_sem.at[2]),
    ]
    for copy in inputs:
        copy.start()
    early = 2
    for i in range(early):
        adj_copy(i).start()

    live_count = ncount[0]
    used = tcount[0]

    lane = lax.broadcasted_iota(jnp.int32, (8, TILE), 1)
    for copy in inputs:
        copy.wait()
    for p in range(cols):
        halves = []
        for h in range(2):
            at = (2 * p + h) * TILE
            block = feat_ref[:, at:at + TILE].astype(F32)
            halves.append(jnp.where(lane + at < live_count, block, 0.0))
        fstage[p] = jnp.concatenate(halves, axis=0).astype(BF)
    whalf = weight_ref.shape[1] // 2
    w32 = weight_ref[...].astype(F32)
    wstage[...] = jnp.concatenate([w32[:, :whalf], w32[:, whalf:]], axis=0).astype(BF)

    pl.semaphore_wait(barrier, rows + cols - 2)

    def to_col(phase, source, target):
        def one(k, carry):
            peer = lax.rem(me_c + k, cols)
            pltpu.make_async_remote_copy(
                src_ref=source(peer), dst_ref=target, send_sem=send_sem.at[phase], recv_sem=recv_sem.at[phase],
                device_id=(me_r, peer), device_id_type=MESH,
            ).start()
            return carry

        lax.fori_loop(1, cols, one, 0)

    def to_row(phase, source, target):
        def one(k, carry):
            peer = lax.rem(me_r + k, rows)
            pltpu.make_async_remote_copy(
                src_ref=source(peer), dst_ref=target, send_sem=send_sem.at[phase], recv_sem=recv_sem.at[phase],
                device_id=(peer, me_c), device_id_type=MESH,
            ).start()
            return carry

        lax.fori_loop(1, rows, one, 0)

    def arrived(phase, ref):
        pltpu.make_async_copy(ref, ref, recv_sem.at[phase]).wait()

    def sent(phase, ref):
        pltpu.make_async_copy(ref, ref, send_sem.at[phase]).wait()

    def unstack(ref):
        x = ref[...].astype(F32)
        width = x.shape[2]
        sides = [x[:, :8].reshape(-1, width), x[:, 8:].reshape(-1, width)]
        return jnp.concatenate(sides, axis=1).astype(BF)

    def slice_cols(index):
        return pl.ds(pl.multiple_of(index * 2 * TILE, 2 * TILE), 2 * TILE)

    to_col(0, lambda d: cot_ref.at[:, slice_cols(d)], cgath.at[me_c])
    to_col(1, lambda d: wstage, wgath.at[me_c])
    to_row(2, lambda d: fstage, fgath.at[me_r])
    for i in range(early, chunks):
        adj_copy(i).start()
    own_c = pltpu.make_async_copy(cot_ref.at[:, slice_cols(me_c)], cgath.at[me_c], own_sem.at[0])
    own_w = pltpu.make_async_copy(wstage, wgath.at[me_c], own_sem.at[1])
    own_f = pltpu.make_async_copy(fstage, fgath.at[me_r], own_sem.at[2])
    own_c.start()
    own_w.start()
    own_f.start()

    slot_used = lax.broadcasted_iota(jnp.int32, (1, slots), 1) < used
    key_c = jnp.where(slot_used, tcol_v[...].reshape(1, slots), -1)
    key_r = jnp.where(slot_used, trow_v[...].reshape(1, slots), -1)
    chosen_c[...] = (
        lax.broadcasted_iota(jnp.int32, (rows * tiles_dev, slots), 0) == key_c
    ).astype(F32).astype(BF)
    chosen_r[...] = (lax.broadcasted_iota(jnp.int32, (tiles_dev, slots), 0) == key_r).astype(F32).astype(BF)

    own_c.wait()
    own_w.wait()
    arrived(0, cgath.at[pl.ds(0, cols - 1)])
    arrived(1, wgath.at[pl.ds(0, cols - 1)])
    whole_w = unstack(wgath)
    cot_nodes = cgath[...].reshape(cols * 16, 2 * TILE)
    back = lax.dot_general(whole_w, cot_nodes, NN, preferred_element_type=F32)
    node = lax.broadcasted_iota(jnp.int32, back.shape, 1) + me_c * (2 * TILE)
    back = jnp.where(node < live_count, back, 0.0)
    for d in range(cols):
        part = back[8 * d:8 * d + 8]
        bstage[d] = jnp.concatenate([part[:, :TILE], part[:, TILE:]], axis=0).astype(BF)
    to_col(3, lambda d: bstage.at[d], bgath.at[me_c])
    own_b = pltpu.make_async_copy(bstage.at[me_c], bgath.at[me_c], own_sem.at[3])
    own_b.start()
    zero = jnp.zeros((16, TILE), BF)

    def tile_pass(source, index_s, forward):
        group = 4 * unroll

        def step(g, carry):
            for u in range(unroll):
                s = pl.multiple_of(g * group, group) + 4 * u
                at = [index_s[s + i] for i in range(4)]
                x = [source[at[i] // 2] for i in range(4)]
                spread = (
                    [[x[0], zero], [x[1], zero], [zero, x[2]], [zero, x[3]]]
                    if forward
                    else [[x[0], zero], [zero, x[1]], [x[2], zero], [zero, x[3]]]
                )
                left = jnp.concatenate([jnp.concatenate(pair, axis=1) for pair in spread], axis=0)
                right = jnp.concatenate(
                    [adj[pl.ds(s, 2)].reshape(2 * TILE, TILE), adj[pl.ds(s + 2, 2)].reshape(2 * TILE, TILE)], axis=1
                )
                out = lax.dot_general(left, right, NT if forward else NN, preferred_element_type=F32)
                for i in range(4):
                    half = i % 2 if forward else i // 2
                    block = out[16 * i:16 * i + 16, TILE * half:TILE * half + TILE]
                    block = jnp.where(at[i] % 2 == 0, block[:8], block[8:])
                    block = jnp.where(s + i < used, block, 0.0)
                    prod[pl.ds(pl.multiple_of((s + i) * 8, 8), 8), :] = block
            return carry

        return step

    def add_up(chosen, tiles):
        picks = chosen[...]
        for f in range(0, 8, 2):
            pair = jnp.concatenate([prod[pl.ds(f + j, slots, stride=8), :] for j in range(2)], axis=1)
            high = pair.astype(BF)
            low = (pair - high.astype(F32)).astype(BF)
            total = lax.dot_general(picks, high, NN, preferred_element_type=F32) + lax.dot_general(
                picks, low, NN, preferred_element_type=F32
            )
            for j in range(2):
                sums[pl.ds(f + j, tiles, stride=8), :] = total[:, TILE * j:TILE * j + TILE]

    own_f.wait()
    arrived(2, fgath.at[pl.ds(0, rows - 1)])
    features = fgath.reshape(rows * cols, 16, TILE)
    groups = slots // (4 * unroll)
    forward = tile_pass(features, tcol_s, True)

    def forward_step(g, carry):
        adj_copy(g).wait()
        return forward(g, carry)

    lax.fori_loop(0, groups, forward_step, 0)
    add_up(chosen_r, tiles_dev)
    for d in range(cols):
        halves = []
        for h in range(2):
            at = 2 * d + h
            block = sums[8 * at:8 * at + 8, :]
            halves.append(jnp.where(lane + at * TILE < live_count, block, 0.0))
        astage[d] = jnp.concatenate(halves, axis=0).astype(BF)
    to_col(5, lambda d: astage.at[d], agath.at[me_c])
    own_a = pltpu.make_async_copy(astage.at[me_c], agath.at[me_c], own_sem.at[5])
    own_a.start()
    own_b.wait()
    arrived(3, bgath.at[pl.ds(0, cols - 1)])

    backward = tile_pass(bgath, trow_s, False)
    lax.fori_loop(0, groups - 1, backward, 0)
    own_a.wait()
    arrived(5, agath.at[pl.ds(0, cols - 1)])

    agg = unstack(agath)
    gw = lax.dot_general(agg, cgath[...].reshape(cols * 16, 2 * TILE), NT, preferred_element_type=F32)
    wpart[...] = gw.reshape(cols, 8, gw.shape[1])
    to_col(6, lambda d: wpart.at[d], wpgath.at[me_c])
    whole_w = unstack(wgath)
    hidden = lax.dot_general(whole_w, agg, (((0,), (0,)), ((), ())), preferred_element_type=F32)
    hstage[...] = hidden.astype(BF).reshape(cols, 16, 2 * TILE)
    to_col(7, lambda d: hstage.at[d], hid_ref.at[:, slice_cols(me_c)])
    own_h = pltpu.make_async_copy(hstage.at[me_c], hid_ref.at[:, slice_cols(me_c)], own_sem.at[6])
    own_h.start()
    own_p = pltpu.make_async_copy(wpart.at[me_c], wpgath.at[me_c], own_sem.at[7])
    own_p.start()

    lax.fori_loop(groups - 1, groups, backward, 0)
    add_up(chosen_c, rows * tiles_dev)
    for d in range(rows):
        size = tiles_dev * 8
        gstage[d] = sums[d * size:(d + 1) * size, :].reshape(cols, 16, TILE).astype(BF)
    to_row(4, lambda d: gstage.at[d], ggath.at[me_r])
    own_g = pltpu.make_async_copy(gstage.at[me_r], ggath.at[me_r], own_sem.at[4])
    own_g.start()

    own_p.wait()
    arrived(6, wpgath.at[pl.ds(0, cols - 1)])
    wrow[...] = jnp.sum(wpgath[...], axis=0)
    to_row(8, lambda d: wrow, wrgath.at[me_r])
    own_r = pltpu.make_async_copy(wrow, wrgath.at[me_r], own_sem.at[8])
    own_r.start()
    own_g.wait()
    arrived(4, ggath.at[pl.ds(0, rows - 1)])
    for p in range(cols):
        total = ggath[0, p].astype(F32)
        for d in range(1, rows):
            total = total + ggath[d, p].astype(F32)
        for h in range(2):
            at = (2 * p + h) * TILE
            gf_ref[:, at:at + TILE] = jnp.where(lane + at < live_count, total[8 * h:8 * h + 8], 0.0).astype(BF)

    own_r.wait()
    arrived(8, wrgath.at[pl.ds(0, rows - 1)])
    total = wrgath[0]
    for d in range(1, rows):
        total = total + wrgath[d]
    gw_ref[...] = total * float(node_total) ** (-0.5)

    own_h.wait()
    arrived(7, hstage.at[pl.ds(0, cols - 1)])
    sent(0, cgath.at[pl.ds(0, cols - 1)])
    sent(1, wgath.at[pl.ds(0, cols - 1)])
    sent(2, fgath.at[pl.ds(0, rows - 1)])
    sent(3, bgath.at[pl.ds(0, cols - 1)])
    sent(4, ggath.at[pl.ds(0, rows - 1)])
    sent(5, agath.at[pl.ds(0, cols - 1)])
    sent(6, wpgath.at[pl.ds(0, cols - 1)])
    sent(7, hstage.at[pl.ds(0, cols - 1)])
    sent(8, wrgath.at[pl.ds(0, rows - 1)])


def finish(a_in, b_in, c_in, a_out, b_out, c_out):
    a_out[...] = a_in[...]
    b_out[...] = b_in[...]
    c_out[...] = c_in[...]


def solution(mesh):
    rows, cols = mesh.shape["row"], mesh.shape["col"]

    def local(features, weight, cotangent, adjacency, tile_rows, tile_cols, tile_count, node_count):
        slots = adjacency.shape[0]
        feats, nodes = features.shape
        hid = weight.shape[1]
        tiles = nodes // TILE
        unroll = 20
        groups = slots // (4 * unroll)
        smem = pl.BlockSpec(memory_space=pltpu.SMEM)
        vmem = pl.BlockSpec(memory_space=pltpu.VMEM)
        anywhere = pl.BlockSpec(memory_space=pl.ANY)
        partial_out = pl.pallas_call(
            functools.partial(kernel, rows, cols, slots, groups, unroll),
            out_shape=(
                jax.ShapeDtypeStruct(cotangent.shape, BF),
                jax.ShapeDtypeStruct(weight.shape, F32),
                jax.ShapeDtypeStruct(features.shape, BF),
            ),
            in_specs=[anywhere] * 4 + [smem, smem, vmem, vmem, smem, smem],
            out_specs=(vmem, vmem, vmem),
            scratch_shapes=[
                pltpu.VMEM(features.shape, BF),
                pltpu.VMEM(weight.shape, BF),
                pltpu.VMEM(cotangent.shape, BF),
                pltpu.VMEM((slots, TILE, TILE), BF),
                pltpu.VMEM((cols, 16, TILE), BF),
                pltpu.VMEM((rows, cols, 16, TILE), BF),
                pltpu.VMEM((cols, 16, 2 * TILE), BF),
                pltpu.VMEM((16, hid // 2), BF),
                pltpu.VMEM((cols, 16, hid // 2), BF),
                pltpu.VMEM((cols, 16, TILE), BF),
                pltpu.VMEM((cols, 16, TILE), BF),
                pltpu.VMEM((slots * 8, TILE), F32),
                pltpu.VMEM((rows * tiles * 8, TILE), F32),
                pltpu.VMEM((rows, cols, 16, TILE), BF),
                pltpu.VMEM((rows, cols, 16, TILE), BF),
                pltpu.VMEM((cols, 16, TILE), BF),
                pltpu.VMEM((cols, 16, TILE), BF),
                pltpu.VMEM((cols, 16, 2 * TILE), BF),
                pltpu.VMEM((cols, 8, hid), F32),
                pltpu.VMEM((cols, 8, hid), F32),
                pltpu.VMEM((8, hid), F32),
                pltpu.VMEM((rows, 8, hid), F32),
                pltpu.VMEM((rows * tiles, slots), BF),
                pltpu.VMEM((tiles, slots), BF),
                pltpu.SemaphoreType.DMA((groups,)),
                pltpu.SemaphoreType.DMA((3,)),
                pltpu.SemaphoreType.DMA((9,)),
                pltpu.SemaphoreType.DMA((9,)),
                pltpu.SemaphoreType.DMA((9,)),
            ],
            compiler_params=pltpu.CompilerParams(
                collective_id=0, has_side_effects=True, vmem_limit_bytes=60 * 2**20
            ),
        )(
            features, weight, cotangent, adjacency, tile_rows, tile_cols,
            tile_rows, tile_cols, tile_count, node_count,
        )
        return pl.pallas_call(
            finish,
            out_shape=[jax.ShapeDtypeStruct(x.shape, x.dtype) for x in partial_out],
            in_specs=[vmem] * 3,
            out_specs=[vmem] * 3,
        )(*partial_out)

    return jax.shard_map(
        local,
        mesh=mesh,
        in_specs=(
            P("col", "row"), P("col", None), P("col", "row"), P("row", None, None),
            P("row"), P("row"), P("row"), P("row"),
        ),
        out_specs=(P("col", "row"), P("col", None), P("col", "row")),
        check_vma=False,
    )
```

```python
import functools

import jax
import jax.numpy as jnp
from jax import lax
from jax.experimental import pallas as pl
from jax.experimental.pallas import tpu as pltpu
from jax.sharding import PartitionSpec as P

TILE = 128
MESH = pl.DeviceIdType.MESH
NT = (((1,), (1,)), ((), ()))
NN = (((1,), (0,)), ((), ()))
BF = jnp.bfloat16
F32 = jnp.float32


def kernel(
    rows, cols, slots, chunks, unroll,
    feat_hbm, weight_hbm, cot_hbm, adj_hbm, trow_s, tcol_s, trow_v, tcol_v, tcount, ncount,
    hid_ref, gw_ref, gf_ref,
    feat_ref, weight_ref, cot_ref, adj, fstage, fgath, cgath, wstage, wgath, bstage, bgath, bsib, cline,
    prod, pown, gsib, grecv, gstage, ggath, gsum,
    astage, agath, apart, hstage, wpart, wfinal, chosen_c, chosen_r,
    adj_sem, in_sem, own_sem, send_sem, recv_sem, pair_send, pair_recv, grad_sem,
):
    me_r = lax.axis_index("row")
    me_c = lax.axis_index("col")
    core = lax.rem(me_c, 2)
    sibling = me_c + 1 - 2 * core
    line = me_c // 4
    side_x = lax.rem(me_c // 2, 2)
    partner = me_c + 2 - 4 * side_x
    tiles_dev = 2 * cols
    tiles_all = rows * tiles_dev
    node_total = tiles_all * TILE
    half = slots // 2
    base = core * half
    per_chunk = slots // chunks

    def adj_copy(i):
        part = pl.ds(i * per_chunk, per_chunk)
        return pltpu.make_async_copy(adj_hbm.at[part], adj.at[part], adj_sem.at[i])

    barrier = pltpu.get_barrier_semaphore()

    def greet_row(k, carry):
        pl.semaphore_signal(barrier, inc=1, device_id=(lax.rem(me_r + k, rows), me_c), device_id_type=MESH)
        return carry

    def greet_col(k, carry):
        pl.semaphore_signal(barrier, inc=1, device_id=(me_r, lax.rem(me_c + k, cols)), device_id_type=MESH)
        return carry

    def greet_partner(k, carry):
        pl.semaphore_signal(barrier, inc=1, device_id=(lax.rem(me_r + k, rows), partner), device_id_type=MESH)
        return carry

    lax.fori_loop(1, rows, greet_row, 0)
    lax.fori_loop(1, rows, greet_partner, 0)
    lax.fori_loop(1, cols, greet_col, 0)

    inputs = [
        pltpu.make_async_copy(feat_hbm, feat_ref, in_sem.at[0]),
        pltpu.make_async_copy(cot_hbm, cot_ref, in_sem.at[1]),
        pltpu.make_async_copy(weight_hbm, weight_ref, in_sem.at[2]),
    ]
    for copy in inputs:
        copy.start()
    early = 2
    for i in range(early):
        adj_copy(i).start()

    live_count = ncount[0]
    used = tcount[0]

    lane = lax.broadcasted_iota(jnp.int32, (8, TILE), 1)
    for copy in inputs:
        copy.wait()
    for p in range(cols):
        halves = []
        for h in range(2):
            at = (2 * p + h) * TILE
            block = feat_ref[:, at:at + TILE].astype(F32)
            halves.append(jnp.where(lane + at < live_count, block, 0.0))
        fstage[p] = jnp.concatenate(halves, axis=0).astype(BF)
    whalf = weight_ref.shape[1] // 2
    w32 = weight_ref[...].astype(F32)
    wstage[...] = jnp.concatenate([w32[:, :whalf], w32[:, whalf:]], axis=0).astype(BF)

    pl.semaphore_wait(barrier, 2 * rows + cols - 3)

    def to_col(phase, source, target):
        def one(k, carry):
            peer = lax.rem(me_c + k, cols)
            pltpu.make_async_remote_copy(
                src_ref=source(peer), dst_ref=target, send_sem=send_sem.at[phase], recv_sem=recv_sem.at[phase],
                device_id=(me_r, peer), device_id_type=MESH,
            ).start()
            return carry

        lax.fori_loop(1, cols, one, 0)

    def to_row(phase, source, target):
        def one(k, carry):
            peer = lax.rem(me_r + k, rows)
            pltpu.make_async_remote_copy(
                src_ref=source(peer), dst_ref=target, send_sem=send_sem.at[phase], recv_sem=recv_sem.at[phase],
                device_id=(peer, me_c), device_id_type=MESH,
            ).start()
            return carry

        lax.fori_loop(1, rows, one, 0)

    def to_pair(phase, source, target):
        pltpu.make_async_remote_copy(
            src_ref=source, dst_ref=target, send_sem=pair_send.at[phase], recv_sem=pair_recv.at[phase],
            device_id=(me_r, sibling), device_id_type=MESH,
        ).start()

    def arrived(phase, ref):
        pltpu.make_async_copy(ref, ref, recv_sem.at[phase]).wait()

    def sent(phase, ref):
        pltpu.make_async_copy(ref, ref, send_sem.at[phase]).wait()

    def pair_arrived(phase, ref):
        pltpu.make_async_copy(ref, ref, pair_recv.at[phase]).wait()

    def pair_sent(phase, ref):
        pltpu.make_async_copy(ref, ref, pair_send.at[phase]).wait()

    def unstack(ref):
        x = ref[...].astype(F32)
        width = x.shape[2]
        sides = [x[:, :8].reshape(-1, width), x[:, 8:].reshape(-1, width)]
        return jnp.concatenate(sides, axis=1).astype(BF)

    def slice_cols(index):
        return pl.ds(pl.multiple_of(index * 2 * TILE, 2 * TILE), 2 * TILE)

    to_col(0, lambda d: cot_ref.at[:, slice_cols(d)], cgath.at[me_c])
    to_col(1, lambda d: wstage, wgath.at[me_c])
    to_row(2, lambda d: fstage, fgath.at[me_r])
    for k in range(1, 4):
        pltpu.make_async_remote_copy(
            src_ref=cot_ref, dst_ref=cline.at[line, core], send_sem=send_sem.at[8], recv_sem=recv_sem.at[8],
            device_id=(me_r, lax.rem(me_c + 4 * k, cols)), device_id_type=MESH,
        ).start()
    for i in range(early, chunks):
        adj_copy(i).start()
    own_c = pltpu.make_async_copy(cot_ref.at[:, slice_cols(me_c)], cgath.at[me_c], own_sem.at[0])
    own_w = pltpu.make_async_copy(wstage, wgath.at[me_c], own_sem.at[1])
    own_f = pltpu.make_async_copy(fstage, fgath.at[me_r], own_sem.at[2])
    own_c.start()
    own_w.start()
    own_f.start()
    own_l = pltpu.make_async_copy(cot_ref, cline.at[line, core], own_sem.at[4])
    own_l.start()

    slot = lax.broadcasted_iota(jnp.int32, (1, slots), 1)
    key_r = jnp.where(slot < used, trow_v[...].reshape(1, slots), -1)
    key_c = jnp.where(slot < used, tcol_v[...].reshape(1, slots), -1)
    key_c = jnp.where(core == 0, key_c[:, :half], key_c[:, half:])
    chosen_c[...] = (lax.broadcasted_iota(jnp.int32, (tiles_all, half), 0) == key_c).astype(F32).astype(BF)
    chosen_r[...] = (lax.broadcasted_iota(jnp.int32, (tiles_dev, slots), 0) == key_r).astype(F32).astype(BF)

    own_c.wait()
    own_w.wait()
    arrived(0, cgath.at[pl.ds(0, cols - 1)])
    arrived(1, wgath.at[pl.ds(0, cols - 1)])
    whole_w = unstack(wgath)
    cot_nodes = cgath[...].reshape(cols * 16, 2 * TILE)
    back = lax.dot_general(whole_w, cot_nodes, NN, preferred_element_type=F32)
    node = lax.broadcasted_iota(jnp.int32, back.shape, 1) + me_c * (2 * TILE)
    back = jnp.where(node < live_count, back, 0.0)
    for d in range(cols):
        part = back[8 * d:8 * d + 8]
        bstage[d] = jnp.concatenate([part[:, :TILE], part[:, TILE:]], axis=0).astype(BF)
    to_col(3, lambda d: bstage.at[d], bgath.at[me_c])
    own_b = pltpu.make_async_copy(bstage.at[me_c], bgath.at[me_c], own_sem.at[3])
    own_b.start()

    def tile_pass(sources, index_s, first, size, forward):
        group = 4 * unroll
        count = len(sources)
        depth = 16 * count
        zero = jnp.zeros((depth, TILE), BF)

        def step(g, carry):
            for u in range(unroll):
                s = pl.multiple_of(g * group, group) + 4 * u
                at = [index_s[first + s + i] for i in range(4)]
                x = [jnp.concatenate([ref[at[i] // 2] for ref in sources], axis=0) for i in range(4)]
                spread = (
                    [[x[0], zero], [x[1], zero], [zero, x[2]], [zero, x[3]]]
                    if forward
                    else [[x[0], zero], [zero, x[1]], [x[2], zero], [zero, x[3]]]
                )
                left = jnp.concatenate([jnp.concatenate(pair, axis=1) for pair in spread], axis=0)
                tiles = [adj[pl.ds(first + s + 2 * i, 2)].reshape(2 * TILE, TILE) for i in range(2)]
                right = jnp.concatenate(tiles, axis=1)
                out = lax.dot_general(left, right, NT if forward else NN, preferred_element_type=F32)
                for i in range(4):
                    side = i % 2 if forward else i // 2
                    for j in range(count):
                        top = depth * i + 16 * j
                        block = out[top:top + 16, TILE * side:TILE * side + TILE]
                        block = jnp.where(at[i] % 2 == 0, block[:8], block[8:])
                        block = jnp.where(first + s + i < used, block, 0.0)
                        prod[pl.ds(pl.multiple_of((j * size + s + i) * 8, 8), 8), :] = block
            return carry

        return step

    def add_up(chosen, which, size, take, pairs=range(4)):
        picks = chosen[...]
        for f in [2 * p for p in pairs]:
            top = which * size * 8 + f
            pair = jnp.concatenate([prod[pl.ds(top + j, size, stride=8), :] for j in range(2)], axis=1)
            high = pair.astype(BF)
            low = (pair - high.astype(F32)).astype(BF)
            total = lax.dot_general(picks, high, NN, preferred_element_type=F32) + lax.dot_general(
                picks, low, NN, preferred_element_type=F32
            )
            for j in range(2):
                take(f + j, total[:, TILE * j:TILE * j + TILE])

    own_f.wait()
    arrived(2, fgath.at[pl.ds(0, rows - 1)])
    groups = slots // (4 * unroll)
    late = groups - 2
    forward = tile_pass([fgath.reshape(rows * cols, 16, TILE)], tcol_s, 0, slots, True)

    def forward_step(g, carry):
        adj_copy(g).wait()
        return forward(g, carry)

    lax.fori_loop(0, late, forward_step, 0)
    own_b.wait()
    arrived(3, bgath.at[pl.ds(0, cols - 1)])
    to_pair(1, bgath, bsib)
    own_l.wait()
    arrived(8, cline.at[pl.ds(0, 3), 0])
    to_pair(0, cline.at[:, core], cline.at[:, core])
    lax.fori_loop(late, groups, forward_step, 0)

    def take_pown(f, block):
        pown[pl.ds(f * tiles_dev, tiles_dev), :] = block

    add_up(chosen_r, 0, slots, take_pown)
    for d in range(cols):
        halves = []
        for h in range(2):
            t = 2 * d + h
            block = pown[pl.ds(t, 8, stride=tiles_dev), :]
            halves.append(jnp.where(lane + t * TILE < live_count, block, 0.0))
        astage[d] = jnp.concatenate(halves, axis=0).astype(BF)
    to_col(5, lambda d: astage.at[d], agath.at[me_c])
    pltpu.make_async_remote_copy(
        src_ref=astage, dst_ref=apart, send_sem=send_sem.at[6], recv_sem=recv_sem.at[6],
        device_id=(me_r, partner), device_id_type=MESH,
    ).start()
    own_a = pltpu.make_async_copy(astage.at[me_c], agath.at[me_c], own_sem.at[5])
    own_a.start()

    pair_arrived(1, bsib)
    backward = tile_pass([bgath, bsib], trow_s, base, half, False)
    lax.fori_loop(0, half // (4 * unroll), backward, 0)

    def take_gsib(f, block):
        gsib[f] = block.astype(BF)
        if f % 2 == 1:
            part = pl.ds(f - 1, 2)
            to_pair(2 + f // 2, gsib.at[part], grecv.at[part])

    def take_gown(f, block):
        if f % 2 == 0:
            pair_arrived(2 + f // 2, grecv.at[pl.ds(f, 2)])
        block = (block + grecv[f].astype(F32)).astype(BF)
        for d in range(rows):
            gstage[d, f] = block[d * tiles_dev:(d + 1) * tiles_dev]

    def to_owners(part):
        here = pl.ds(4 * part, 4)

        def one(k, carry):
            peer = lax.rem(me_r + k, rows)
            pltpu.make_async_remote_copy(
                src_ref=gstage.at[peer, here], dst_ref=ggath.at[me_r, here],
                send_sem=send_sem.at[9], recv_sem=grad_sem.at[part, me_r],
                device_id=(peer, me_c), device_id_type=MESH,
            ).start()
            return carry

        lax.fori_loop(1, rows, one, 0)

    add_up(chosen_c, 1, half, take_gsib, (0, 1, 2))
    pair_arrived(0, cline.at[:, 0])
    arrived(6, astage)
    both = []
    for d in range(cols):
        mine, theirs = astage[d].astype(F32), apart[d].astype(F32)
        for h in range(2):
            both.append(jnp.concatenate([mine[8 * h:8 * h + 8], theirs[8 * h:8 * h + 8]], axis=0).astype(BF))
    left = jnp.concatenate(both, axis=1)
    gw = lax.dot_general(left, cline[...].reshape(cols // 2 * 16, left.shape[1]), NT, preferred_element_type=F32)
    wpart[...] = gw.reshape(2, 8, gw.shape[1])
    wfinal[me_r, side_x] = gw[:8]
    to_row(4, lambda d: wpart.at[0], wfinal.at[me_r, side_x])

    def to_partner(k, carry):
        pltpu.make_async_remote_copy(
            src_ref=wpart.at[1], dst_ref=wfinal.at[me_r, side_x], send_sem=send_sem.at[4], recv_sem=recv_sem.at[4],
            device_id=(lax.rem(me_r + k, rows), partner), device_id_type=MESH,
        ).start()
        return carry

    lax.fori_loop(0, rows, to_partner, 0)

    add_up(chosen_c, 0, half, take_gown, (0, 1))
    to_owners(0)
    add_up(chosen_c, 1, half, take_gsib, (3,))
    add_up(chosen_c, 0, half, take_gown, (2, 3))
    to_owners(1)

    own_a.wait()
    arrived(5, agath.at[pl.ds(0, cols - 1)])
    agg = unstack(agath)
    whole_w = unstack(wgath)
    hidden = lax.dot_general(whole_w, agg, (((0,), (0,)), ((), ())), preferred_element_type=F32)
    hstage[...] = hidden.astype(BF).reshape(cols, 16, 2 * TILE)
    to_col(7, lambda d: hstage.at[d], hid_ref.at[:, slice_cols(me_c)])
    own_h = pltpu.make_async_copy(hstage.at[me_c], hid_ref.at[:, slice_cols(me_c)], own_sem.at[6])
    own_h.start()

    arrived(4, wfinal.reshape(2 * rows, 8, wfinal.shape[3]).at[pl.ds(0, 2 * rows - 1)])
    total = wfinal[0]
    for d in range(1, rows):
        total = total + wfinal[d]
    width = gw.shape[1] // 4
    parts = [total[x, :, y * width:(y + 1) * width] for y in range(4) for x in range(2)]
    gw_ref[...] = jnp.concatenate(parts, axis=1) * float(node_total) ** (-0.5)

    x_me, z_me = me_r // (rows // 2), lax.rem(me_r, rows // 2)
    for part in range(2):
        here = pl.ds(4 * part, 4)
        total = gstage[me_r, here].astype(F32)
        for dx, dz in ((0, 1), (0, 3), (1, 0), (0, 2), (1, 1), (1, 3), (1, 2)):
            source = lax.rem(x_me + dx, 2) * (rows // 2) + lax.rem(z_me + dz, rows // 2)
            block = ggath.at[source, here]
            pltpu.make_async_copy(block, block, grad_sem.at[part, source]).wait()
            total = total + block[...].astype(F32)
        gsum[pl.ds(4 * part * tiles_dev, 4 * tiles_dev), :] = total.reshape(4 * tiles_dev, TILE)
    for t in range(tiles_dev):
        block = gsum[pl.ds(t, 8, stride=tiles_dev), :]
        gf_ref[:, t * TILE:(t + 1) * TILE] = jnp.where(lane + t * TILE < live_count, block, 0.0).astype(BF)

    own_h.wait()
    arrived(7, hstage.at[pl.ds(0, cols - 1)])
    sent(0, cgath.at[pl.ds(0, cols - 1)])
    sent(1, wgath.at[pl.ds(0, cols - 1)])
    sent(2, fgath.at[pl.ds(0, rows - 1)])
    sent(3, bgath.at[pl.ds(0, cols - 1)])
    sent(4, wfinal.reshape(2 * rows, 8, wfinal.shape[3]).at[pl.ds(0, 2 * rows - 1)])
    sent(5, agath.at[pl.ds(0, cols - 1)])
    sent(6, astage)
    sent(7, hstage.at[pl.ds(0, cols - 1)])
    sent(8, cline.at[pl.ds(0, 3), 0])
    sent(9, ggath.at[pl.ds(0, rows - 1)])
    pair_sent(0, cline.at[:, 0])
    pair_sent(1, bsib)
    for i in range(4):
        pair_sent(2 + i, gsib.at[pl.ds(2 * i, 2)])


def finish(a_in, b_in, c_in, a_out, b_out, c_out):
    a_out[...] = a_in[...]
    b_out[...] = b_in[...]
    c_out[...] = c_in[...]


def solution(mesh):
    rows, cols = mesh.shape["row"], mesh.shape["col"]

    def local(features, weight, cotangent, adjacency, tile_rows, tile_cols, tile_count, node_count):
        slots = adjacency.shape[0]
        feats, nodes = features.shape
        hid = weight.shape[1]
        tiles = nodes // TILE
        unroll = 20
        half = slots // 2
        groups = slots // (4 * unroll)
        smem = pl.BlockSpec(memory_space=pltpu.SMEM)
        vmem = pl.BlockSpec(memory_space=pltpu.VMEM)
        anywhere = pl.BlockSpec(memory_space=pl.ANY)
        partial_out = pl.pallas_call(
            functools.partial(kernel, rows, cols, slots, groups, unroll),
            out_shape=(
                jax.ShapeDtypeStruct(cotangent.shape, BF),
                jax.ShapeDtypeStruct(weight.shape, F32),
                jax.ShapeDtypeStruct(features.shape, BF),
            ),
            in_specs=[anywhere] * 4 + [smem, smem, vmem, vmem, smem, smem],
            out_specs=(vmem, vmem, vmem),
            scratch_shapes=[
                pltpu.VMEM(features.shape, BF),
                pltpu.VMEM(weight.shape, BF),
                pltpu.VMEM(cotangent.shape, BF),
                pltpu.VMEM((slots, TILE, TILE), BF),
                pltpu.VMEM((cols, 16, TILE), BF),
                pltpu.VMEM((rows, cols, 16, TILE), BF),
                pltpu.VMEM((cols, 16, 2 * TILE), BF),
                pltpu.VMEM((16, hid // 2), BF),
                pltpu.VMEM((cols, 16, hid // 2), BF),
                pltpu.VMEM((cols, 16, TILE), BF),
                pltpu.VMEM((cols, 16, TILE), BF),
                pltpu.VMEM((cols, 16, TILE), BF),
                pltpu.VMEM((4, 2) + cotangent.shape, BF),
                pltpu.VMEM((slots * 8, TILE), F32),
                pltpu.VMEM((8 * tiles, TILE), F32),
                pltpu.VMEM((8, rows * tiles, TILE), BF),
                pltpu.VMEM((8, rows * tiles, TILE), BF),
                pltpu.VMEM((rows, 8, tiles, TILE), BF),
                pltpu.VMEM((rows, 8, tiles, TILE), BF),
                pltpu.VMEM((8 * tiles, TILE), F32),
                pltpu.VMEM((cols, 16, TILE), BF),
                pltpu.VMEM((cols, 16, TILE), BF),
                pltpu.VMEM((cols, 16, TILE), BF),
                pltpu.VMEM((cols, 16, 2 * TILE), BF),
                pltpu.VMEM((2, 8, hid // 2), F32),
                pltpu.VMEM((rows, 2, 8, hid // 2), F32),
                pltpu.VMEM((rows * tiles, half), BF),
                pltpu.VMEM((tiles, slots), BF),
                pltpu.SemaphoreType.DMA((groups,)),
                pltpu.SemaphoreType.DMA((3,)),
                pltpu.SemaphoreType.DMA((8,)),
                pltpu.SemaphoreType.DMA((10,)),
                pltpu.SemaphoreType.DMA((10,)),
                pltpu.SemaphoreType.DMA((6,)),
                pltpu.SemaphoreType.DMA((6,)),
                pltpu.SemaphoreType.DMA((2, rows)),
            ],
            compiler_params=pltpu.CompilerParams(
                collective_id=0, has_side_effects=True, vmem_limit_bytes=60 * 2**20
            ),
        )(
            features, weight, cotangent, adjacency, tile_rows, tile_cols,
            tile_rows, tile_cols, tile_count, node_count,
        )
        return pl.pallas_call(
            finish,
            out_shape=[jax.ShapeDtypeStruct(x.shape, x.dtype) for x in partial_out],
            in_specs=[vmem] * 3,
            out_specs=[vmem] * 3,
        )(*partial_out)

    return jax.shard_map(
        local,
        mesh=mesh,
        in_specs=(
            P("col", "row"), P("col", None), P("col", "row"), P("row", None, None),
            P("row"), P("row"), P("row"), P("row"),
        ),
        out_specs=(P("col", "row"), P("col", None), P("col", "row")),
        check_vma=False,
    )
```

```python
import functools

import jax
import jax.numpy as jnp
from jax import lax
from jax.experimental import pallas as pl
from jax.experimental.pallas import tpu as pltpu
from jax.sharding import PartitionSpec as P

TILE = 128
MESH = pl.DeviceIdType.MESH
NT = (((1,), (1,)), ((), ()))
NN = (((1,), (0,)), ((), ()))
BF = jnp.bfloat16
F32 = jnp.float32


def kernel(
    rows, cols, slots, chunks, unroll,
    feat_hbm, weight_hbm, cot_hbm, adj_hbm, trow_s, tcol_s, trow_v, tcol_v, tcount, ncount,
    hid_ref, gw_ref, gf_ref,
    feat_ref, weight_ref, cot_ref, adj, fstage, fgath, cgath, wstage, wgath, bstage, bgath, bsib, cline,
    prod, pown, gsib, grecv, gstage, ggath, ends_v, ends,
    astage, agath, apart, hstage, wpart, wfinal, chosen_r,
    adj_sem, in_sem, own_sem, send_sem, recv_sem, pair_send, pair_recv, grad_sem,
):
    me_r = lax.axis_index("row")
    me_c = lax.axis_index("col")
    core = lax.rem(me_c, 2)
    sibling = me_c + 1 - 2 * core
    line = me_c // 4
    side_x = lax.rem(me_c // 2, 2)
    partner = me_c + 2 - 4 * side_x
    tiles_dev = 2 * cols
    tiles_all = rows * tiles_dev
    node_total = tiles_all * TILE
    half = slots // 2
    base = core * half
    per_chunk = slots // chunks

    def adj_copy(i):
        part = pl.ds(i * per_chunk, per_chunk)
        return pltpu.make_async_copy(adj_hbm.at[part], adj.at[part], adj_sem.at[i])

    barrier = pltpu.get_barrier_semaphore()

    def greet_row(k, carry):
        pl.semaphore_signal(barrier, inc=1, device_id=(lax.rem(me_r + k, rows), me_c), device_id_type=MESH)
        return carry

    def greet_col(k, carry):
        pl.semaphore_signal(barrier, inc=1, device_id=(me_r, lax.rem(me_c + k, cols)), device_id_type=MESH)
        return carry

    def greet_partner(k, carry):
        pl.semaphore_signal(barrier, inc=1, device_id=(lax.rem(me_r + k, rows), partner), device_id_type=MESH)
        return carry

    lax.fori_loop(1, rows, greet_row, 0)
    lax.fori_loop(1, rows, greet_partner, 0)
    lax.fori_loop(1, cols, greet_col, 0)

    inputs = [
        pltpu.make_async_copy(feat_hbm, feat_ref, in_sem.at[0]),
        pltpu.make_async_copy(cot_hbm, cot_ref, in_sem.at[1]),
        pltpu.make_async_copy(weight_hbm, weight_ref, in_sem.at[2]),
    ]
    for copy in inputs:
        copy.start()
    early = 2
    for i in range(early):
        adj_copy(i).start()

    live_count = ncount[0]
    used = tcount[0]

    lane = lax.broadcasted_iota(jnp.int32, (8, TILE), 1)
    for copy in inputs:
        copy.wait()
    for p in range(cols):
        halves = []
        for h in range(2):
            at = (2 * p + h) * TILE
            block = feat_ref[:, at:at + TILE].astype(F32)
            halves.append(jnp.where(lane + at < live_count, block, 0.0))
        fstage[p] = jnp.concatenate(halves, axis=0).astype(BF)
    whalf = weight_ref.shape[1] // 2
    w32 = weight_ref[...].astype(F32)
    wstage[...] = jnp.concatenate([w32[:, :whalf], w32[:, whalf:]], axis=0).astype(BF)

    pl.semaphore_wait(barrier, 2 * rows + cols - 3)

    def to_col(phase, source, target):
        def one(k, carry):
            peer = lax.rem(me_c + k, cols)
            pltpu.make_async_remote_copy(
                src_ref=source(peer), dst_ref=target, send_sem=send_sem.at[phase], recv_sem=recv_sem.at[phase],
                device_id=(me_r, peer), device_id_type=MESH,
            ).start()
            return carry

        lax.fori_loop(1, cols, one, 0)

    def to_row(phase, source, target):
        def one(k, carry):
            peer = lax.rem(me_r + k, rows)
            pltpu.make_async_remote_copy(
                src_ref=source(peer), dst_ref=target, send_sem=send_sem.at[phase], recv_sem=recv_sem.at[phase],
                device_id=(peer, me_c), device_id_type=MESH,
            ).start()
            return carry

        lax.fori_loop(1, rows, one, 0)

    def to_pair(phase, source, target):
        pltpu.make_async_remote_copy(
            src_ref=source, dst_ref=target, send_sem=pair_send.at[phase], recv_sem=pair_recv.at[phase],
            device_id=(me_r, sibling), device_id_type=MESH,
        ).start()

    def arrived(phase, ref):
        pltpu.make_async_copy(ref, ref, recv_sem.at[phase]).wait()

    def sent(phase, ref):
        pltpu.make_async_copy(ref, ref, send_sem.at[phase]).wait()

    def pair_arrived(phase, ref):
        pltpu.make_async_copy(ref, ref, pair_recv.at[phase]).wait()

    def pair_sent(phase, ref):
        pltpu.make_async_copy(ref, ref, pair_send.at[phase]).wait()

    def unstack(ref):
        x = ref[...].astype(F32)
        width = x.shape[2]
        sides = [x[:, :8].reshape(-1, width), x[:, 8:].reshape(-1, width)]
        return jnp.concatenate(sides, axis=1).astype(BF)

    def slice_cols(index):
        return pl.ds(pl.multiple_of(index * 2 * TILE, 2 * TILE), 2 * TILE)

    to_col(0, lambda d: cot_ref.at[:, slice_cols(d)], cgath.at[me_c])
    to_col(1, lambda d: wstage, wgath.at[me_c])
    to_row(2, lambda d: fstage, fgath.at[me_r])
    for k in range(1, 4):
        pltpu.make_async_remote_copy(
            src_ref=cot_ref, dst_ref=cline.at[line, core], send_sem=send_sem.at[8], recv_sem=recv_sem.at[8],
            device_id=(me_r, lax.rem(me_c + 4 * k, cols)), device_id_type=MESH,
        ).start()
    for i in range(early, chunks):
        adj_copy(i).start()
    own_c = pltpu.make_async_copy(cot_ref.at[:, slice_cols(me_c)], cgath.at[me_c], own_sem.at[0])
    own_w = pltpu.make_async_copy(wstage, wgath.at[me_c], own_sem.at[1])
    own_f = pltpu.make_async_copy(fstage, fgath.at[me_r], own_sem.at[2])
    own_c.start()
    own_w.start()
    own_f.start()
    own_l = pltpu.make_async_copy(cot_ref, cline.at[line, core], own_sem.at[4])
    own_l.start()

    slot = lax.broadcasted_iota(jnp.int32, (1, slots), 1)
    key_r = jnp.where(slot < used, trow_v[...].reshape(1, slots), -1)
    key_c = jnp.where(slot < used, tcol_v[...].reshape(1, slots), tiles_all)
    key_c = jnp.where(core == 0, key_c[:, :half], key_c[:, half:])
    chosen_r[...] = (lax.broadcasted_iota(jnp.int32, (tiles_dev, slots), 0) == key_r).astype(F32).astype(BF)

    tile = lax.broadcasted_iota(jnp.int32, (tiles_all, half), 0)
    upto = jnp.sum((key_c <= tile).astype(jnp.int32), axis=1, keepdims=True)
    below = jnp.sum((key_c < tile).astype(jnp.int32), axis=1, keepdims=True)
    last = jnp.broadcast_to(jnp.where(upto > below, upto - 1, slots), (tiles_all, TILE)).T[:8]
    row = lax.broadcasted_iota(jnp.int32, last.shape, 0)
    ends_v[...] = jnp.where((row == 1) & (last < slots), last + half, last)
    table = pltpu.make_async_copy(ends_v, ends, in_sem.at[3])
    table.start()
    prod[slots] = jnp.zeros((8, TILE), F32)

    own_c.wait()
    own_w.wait()
    arrived(0, cgath.at[pl.ds(0, cols - 1)])
    arrived(1, wgath.at[pl.ds(0, cols - 1)])
    whole_w = unstack(wgath)
    cot_nodes = cgath[...].reshape(cols * 16, 2 * TILE)
    back = lax.dot_general(whole_w, cot_nodes, NN, preferred_element_type=F32)
    node = lax.broadcasted_iota(jnp.int32, back.shape, 1) + me_c * (2 * TILE)
    back = jnp.where(node < live_count, back, 0.0)
    for d in range(cols):
        part = back[8 * d:8 * d + 8]
        bstage[d] = jnp.concatenate([part[:, :TILE], part[:, TILE:]], axis=0).astype(BF)
    to_col(3, lambda d: bstage.at[d], bgath.at[me_c])
    own_b = pltpu.make_async_copy(bstage.at[me_c], bgath.at[me_c], own_sem.at[3])
    own_b.start()
    table.wait()

    def tile_pass(sources, index_s, first, size, forward):
        group = 4 * unroll
        count = len(sources)
        depth = 16 * count
        zero = jnp.zeros((depth, TILE), BF)

        def step(g, runs):
            for u in range(unroll):
                s = pl.multiple_of(g * group, group) + 4 * u
                at = [index_s[first + s + i] for i in range(4)]
                x = [jnp.concatenate([ref[at[i] // 2] for ref in sources], axis=0) for i in range(4)]
                spread = (
                    [[x[0], zero], [x[1], zero], [zero, x[2]], [zero, x[3]]]
                    if forward
                    else [[x[0], zero], [zero, x[1]], [x[2], zero], [zero, x[3]]]
                )
                left = jnp.concatenate([jnp.concatenate(pair, axis=1) for pair in spread], axis=0)
                tiles = [adj[pl.ds(first + s + 2 * i, 2)].reshape(2 * TILE, TILE) for i in range(2)]
                right = jnp.concatenate(tiles, axis=1)
                out = lax.dot_general(left, right, NT if forward else NN, preferred_element_type=F32)
                for i in range(4):
                    side = i % 2 if forward else i // 2
                    for j in range(count):
                        top = depth * i + 16 * j
                        block = out[top:top + 16, TILE * side:TILE * side + TILE]
                        block = jnp.where(at[i] % 2 == 0, block[:8], block[8:])
                        block = jnp.where(first + s + i < used, block, 0.0)
                        if not forward:
                            here = first + s + i
                            same = tcol_s[here] == tcol_s[jnp.maximum(here - 1, 0)]
                            block = block + jnp.where(same, runs[j], 0.0)
                            runs = runs[:j] + (block,) + runs[j + 1:]
                        prod[j * size + s + i] = block
            return runs

        return step

    def add_up(chosen, which, size, take, pairs=range(4)):
        picks = chosen[...]
        flat = prod.reshape((slots + 1) * 8, TILE)
        for f in [2 * p for p in pairs]:
            top = which * size * 8 + f
            pair = jnp.concatenate([flat[pl.ds(top + j, size, stride=8), :] for j in range(2)], axis=1)
            high = pair.astype(BF)
            low = (pair - high.astype(F32)).astype(BF)
            total = lax.dot_general(picks, high, NN, preferred_element_type=F32) + lax.dot_general(
                picks, low, NN, preferred_element_type=F32
            )
            for j in range(2):
                take(f + j, total[:, TILE * j:TILE * j + TILE])

    own_f.wait()
    arrived(2, fgath.at[pl.ds(0, rows - 1)])
    groups = slots // (4 * unroll)
    late = groups - 2
    forward = tile_pass([fgath.reshape(rows * cols, 16, TILE)], tcol_s, 0, slots, True)

    def forward_step(g, carry):
        adj_copy(g).wait()
        return forward(g, carry)

    lax.fori_loop(0, late, forward_step, 0)
    own_b.wait()
    arrived(3, bgath.at[pl.ds(0, cols - 1)])
    to_pair(1, bgath, bsib)
    own_l.wait()
    arrived(8, cline.at[pl.ds(0, 3), 0])
    to_pair(0, cline.at[:, core], cline.at[:, core])
    lax.fori_loop(late, groups, forward_step, 0)

    def take_pown(f, block):
        pown[pl.ds(f * tiles_dev, tiles_dev), :] = block

    add_up(chosen_r, 0, slots, take_pown)
    for d in range(cols):
        halves = []
        for h in range(2):
            t = 2 * d + h
            block = pown[pl.ds(t, 8, stride=tiles_dev), :]
            halves.append(jnp.where(lane + t * TILE < live_count, block, 0.0))
        astage[d] = jnp.concatenate(halves, axis=0).astype(BF)
    to_col(5, lambda d: astage.at[d], agath.at[me_c])
    pltpu.make_async_remote_copy(
        src_ref=astage, dst_ref=apart, send_sem=send_sem.at[6], recv_sem=recv_sem.at[6],
        device_id=(me_r, partner), device_id_type=MESH,
    ).start()
    own_a = pltpu.make_async_copy(astage.at[me_c], agath.at[me_c], own_sem.at[5])
    own_a.start()

    pair_arrived(1, bsib)
    backward = tile_pass([bgath, bsib], trow_s, base, half, False)
    lax.fori_loop(0, half // (4 * unroll), backward, (jnp.zeros((8, TILE), F32),) * 2)

    def gathered(which, d, p):
        t = d * tiles_dev + 2 * p
        return jnp.concatenate([prod[ends[which, t]], prod[ends[which, t + 1]]], axis=0)

    def to_sibling(k, carry):
        d = lax.rem(me_r + k, rows)
        for p in range(cols):
            gsib[d, p] = gathered(1, d, p).astype(BF)
        pltpu.make_async_remote_copy(
            src_ref=gsib.at[d], dst_ref=grecv.at[d], send_sem=pair_send.at[2], recv_sem=pair_recv.at[2 + d],
            device_id=(me_r, sibling), device_id_type=MESH,
        ).start()
        return carry

    lax.fori_loop(1, rows + 1, to_sibling, 0)
    pair_arrived(0, cline.at[:, 0])
    arrived(6, astage)
    both = []
    for d in range(cols):
        mine, theirs = astage[d].astype(F32), apart[d].astype(F32)
        for h in range(2):
            both.append(jnp.concatenate([mine[8 * h:8 * h + 8], theirs[8 * h:8 * h + 8]], axis=0).astype(BF))
    left = jnp.concatenate(both, axis=1)
    gw = lax.dot_general(left, cline[...].reshape(cols // 2 * 16, left.shape[1]), NT, preferred_element_type=F32)
    wpart[...] = gw.reshape(2, 8, gw.shape[1])
    wfinal[me_r, side_x] = gw[:8]
    to_row(4, lambda d: wpart.at[0], wfinal.at[me_r, side_x])

    def to_partner(k, carry):
        pltpu.make_async_remote_copy(
            src_ref=wpart.at[1], dst_ref=wfinal.at[me_r, side_x], send_sem=send_sem.at[4], recv_sem=recv_sem.at[4],
            device_id=(lax.rem(me_r + k, rows), partner), device_id_type=MESH,
        ).start()
        return carry

    lax.fori_loop(0, rows, to_partner, 0)

    def own_share(d):
        pair_arrived(2 + d, grecv.at[d])
        for p in range(cols):
            gstage[d, p] = (gathered(0, d, p) + grecv[d, p].astype(F32)).astype(BF)

    def to_owner(k, carry):
        d = lax.rem(me_r + k, rows)
        own_share(d)
        pltpu.make_async_remote_copy(
            src_ref=gstage.at[d], dst_ref=ggath.at[me_r], send_sem=send_sem.at[9], recv_sem=grad_sem.at[me_r],
            device_id=(d, me_c), device_id_type=MESH,
        ).start()
        return carry

    lax.fori_loop(1, rows, to_owner, 0)
    own_share(me_r)

    own_a.wait()
    arrived(5, agath.at[pl.ds(0, cols - 1)])
    agg = unstack(agath)
    whole_w = unstack(wgath)
    hidden = lax.dot_general(whole_w, agg, (((0,), (0,)), ((), ())), preferred_element_type=F32)
    hstage[...] = hidden.astype(BF).reshape(cols, 16, 2 * TILE)
    to_col(7, lambda d: hstage.at[d], hid_ref.at[:, slice_cols(me_c)])
    own_h = pltpu.make_async_copy(hstage.at[me_c], hid_ref.at[:, slice_cols(me_c)], own_sem.at[6])
    own_h.start()

    arrived(4, wfinal.reshape(2 * rows, 8, wfinal.shape[3]).at[pl.ds(0, 2 * rows - 1)])
    total = wfinal[0]
    for d in range(1, rows):
        total = total + wfinal[d]
    width = gw.shape[1] // 4
    parts = [total[x, :, y * width:(y + 1) * width] for y in range(4) for x in range(2)]
    gw_ref[...] = jnp.concatenate(parts, axis=1) * float(node_total) ** (-0.5)

    x_me, z_me = me_r // (rows // 2), lax.rem(me_r, rows // 2)
    total = gstage[me_r].astype(F32)
    for dx, dz in ((0, 1), (0, 3), (1, 0), (0, 2), (1, 1), (1, 3), (1, 2)):
        source = lax.rem(x_me + dx, 2) * (rows // 2) + lax.rem(z_me + dz, rows // 2)
        block = ggath.at[source]
        pltpu.make_async_copy(block, block, grad_sem.at[source]).wait()
        total = total + block[...].astype(F32)
    for p in range(cols):
        for h in range(2):
            at = (2 * p + h) * TILE
            gf_ref[:, at:at + TILE] = jnp.where(lane + at < live_count, total[p, 8 * h:8 * h + 8], 0.0).astype(BF)

    own_h.wait()
    arrived(7, hstage.at[pl.ds(0, cols - 1)])
    sent(0, cgath.at[pl.ds(0, cols - 1)])
    sent(1, wgath.at[pl.ds(0, cols - 1)])
    sent(2, fgath.at[pl.ds(0, rows - 1)])
    sent(3, bgath.at[pl.ds(0, cols - 1)])
    sent(4, wfinal.reshape(2 * rows, 8, wfinal.shape[3]).at[pl.ds(0, 2 * rows - 1)])
    sent(5, agath.at[pl.ds(0, cols - 1)])
    sent(6, astage)
    sent(7, hstage.at[pl.ds(0, cols - 1)])
    sent(8, cline.at[pl.ds(0, 3), 0])
    sent(9, ggath.at[pl.ds(0, rows - 1)])
    pair_sent(0, cline.at[:, 0])
    pair_sent(1, bsib)
    pair_sent(2, gsib)


def finish(a_in, b_in, c_in, a_out, b_out, c_out):
    a_out[...] = a_in[...]
    b_out[...] = b_in[...]
    c_out[...] = c_in[...]


def solution(mesh):
    rows, cols = mesh.shape["row"], mesh.shape["col"]

    def local(features, weight, cotangent, adjacency, tile_rows, tile_cols, tile_count, node_count):
        slots = adjacency.shape[0]
        feats, nodes = features.shape
        hid = weight.shape[1]
        tiles = nodes // TILE
        unroll = 40
        half = slots // 2
        groups = slots // (4 * unroll)
        smem = pl.BlockSpec(memory_space=pltpu.SMEM)
        vmem = pl.BlockSpec(memory_space=pltpu.VMEM)
        anywhere = pl.BlockSpec(memory_space=pl.ANY)
        partial_out = pl.pallas_call(
            functools.partial(kernel, rows, cols, slots, groups, unroll),
            out_shape=(
                jax.ShapeDtypeStruct(cotangent.shape, BF),
                jax.ShapeDtypeStruct(weight.shape, F32),
                jax.ShapeDtypeStruct(features.shape, BF),
            ),
            in_specs=[anywhere] * 4 + [smem, smem, vmem, vmem, smem, smem],
            out_specs=(vmem, vmem, vmem),
            scratch_shapes=[
                pltpu.VMEM(features.shape, BF),
                pltpu.VMEM(weight.shape, BF),
                pltpu.VMEM(cotangent.shape, BF),
                pltpu.VMEM((slots, TILE, TILE), BF),
                pltpu.VMEM((cols, 16, TILE), BF),
                pltpu.VMEM((rows, cols, 16, TILE), BF),
                pltpu.VMEM((cols, 16, 2 * TILE), BF),
                pltpu.VMEM((16, hid // 2), BF),
                pltpu.VMEM((cols, 16, hid // 2), BF),
                pltpu.VMEM((cols, 16, TILE), BF),
                pltpu.VMEM((cols, 16, TILE), BF),
                pltpu.VMEM((cols, 16, TILE), BF),
                pltpu.VMEM((4, 2) + cotangent.shape, BF),
                pltpu.VMEM((slots + 1, 8, TILE), F32),
                pltpu.VMEM((8 * tiles, TILE), F32),
                pltpu.VMEM((rows, cols, 16, TILE), BF),
                pltpu.VMEM((rows, cols, 16, TILE), BF),
                pltpu.VMEM((rows, cols, 16, TILE), BF),
                pltpu.VMEM((rows, cols, 16, TILE), BF),
                pltpu.VMEM((8, rows * tiles), jnp.int32),
                pltpu.SMEM((8, rows * tiles), jnp.int32),
                pltpu.VMEM((cols, 16, TILE), BF),
                pltpu.VMEM((cols, 16, TILE), BF),
                pltpu.VMEM((cols, 16, TILE), BF),
                pltpu.VMEM((cols, 16, 2 * TILE), BF),
                pltpu.VMEM((2, 8, hid // 2), F32),
                pltpu.VMEM((rows, 2, 8, hid // 2), F32),
                pltpu.VMEM((tiles, slots), BF),
                pltpu.SemaphoreType.DMA((groups,)),
                pltpu.SemaphoreType.DMA((4,)),
                pltpu.SemaphoreType.DMA((8,)),
                pltpu.SemaphoreType.DMA((10,)),
                pltpu.SemaphoreType.DMA((10,)),
                pltpu.SemaphoreType.DMA((3,)),
                pltpu.SemaphoreType.DMA((2 + rows,)),
                pltpu.SemaphoreType.DMA((rows,)),
            ],
            compiler_params=pltpu.CompilerParams(
                collective_id=0, has_side_effects=True, vmem_limit_bytes=60 * 2**20
            ),
        )(
            features, weight, cotangent, adjacency, tile_rows, tile_cols,
            tile_rows, tile_cols, tile_count, node_count,
        )
        return pl.pallas_call(
            finish,
            out_shape=[jax.ShapeDtypeStruct(x.shape, x.dtype) for x in partial_out],
            in_specs=[vmem] * 3,
            out_specs=[vmem] * 3,
        )(*partial_out)

    return jax.shard_map(
        local,
        mesh=mesh,
        in_specs=(
            P("col", "row"), P("col", None), P("col", "row"), P("row", None, None),
            P("row"), P("row"), P("row"), P("row"),
        ),
        out_specs=(P("col", "row"), P("col", None), P("col", "row")),
        check_vma=False,
    )
```
